512 devices in a mesh: gx: 32 (over z, x), gy: 16 (over y, core).
Axes of the slice: x: 4, y: 8, z: 8, core: 2. Of those that a mesh axis runs over, the one named last changes fastest.
Arguments:
- basis: float32 [32, 256, 2048], P(None, 'gx', 'gy'), may hold values from -6 to 6
- search: float32 [32, 256, 2048], P(None, 'gx', 'gy'), may hold values from -6 to 6
- conductivity: float32 [256, 2048], P('gx', 'gy'), may hold values from 0.2 to 5
- rotation: int32 [96, 32], replicated, may hold values from -4 to 4
Outputs:
- new_basis: float32 [32, 256, 2048], P(None, 'gx', 'gy')
- new_search: float32 [32, 256, 2048], P(None, 'gx', 'gy')
- ritz_values: float32 [32], replicated
The draws below stay inside these ranges and needn't reach their ends.
All inputs are finite; a program needn't handle non-finite values.
Results may differ from the reference program's by a relative error of at most 0.0003.
Values sent between devices are 32-bit elements; how exact they have to be, the bound alone decides.
No kernel may reach another device: no remote copies, remote signals or barrier semaphores. Data moves between devices by JAX's collectives and lax.ppermute only.
A program may use at most 64 MiB of HBM per device.

```python
import math
import jax
import jax.numpy as jnp
from jax import lax

K = 32
CZ = 16
NX = 256
NY = 128


def with_ends(array, key, smallest, largest):
    extent = array.shape
    place = [jax.random.randint(jax.random.fold_in(key, axis), (), 0, extent[axis]) for axis in range(len(extent))]
    array = array.at[tuple(place)].set(smallest)
    longest = extent.index(max(extent))
    place[longest] = (place[longest] + 1) % extent[longest]
    return array.at[tuple(place)].set(largest)


def block_scale(key, shape, pieces, low, largest):
    gain = 1.0
    for dim, parts in pieces:
        heights = jax.random.uniform(jax.random.fold_in(jax.random.fold_in(key, 6), dim), (parts,), jnp.float32, low / len(pieces), largest / len(pieces))
        gain = gain * jnp.repeat(jnp.exp(heights), shape[dim] // parts).reshape((-1,) + (1,) * (len(shape) - 1 - dim))
    return gain


def bell_draw(rng, shape, spread, most, shards=(), kind=jnp.bfloat16):
    values = spread * jax.random.normal(rng, shape, jnp.float32)
    if shards:
        values = values * block_scale(rng, shape, shards, -0.22, 0.18)
    return jnp.clip(values, -most, most).astype(kind)


def setup_inputs(seed: int = 0) -> dict:
    key_list = jax.random.split(jax.random.key(seed), 5)
    return {
        "basis": bell_draw(key_list[0], (K, NX, NY * CZ), 1.0, 6.0, ((1, 32), (2, 16)), jnp.float32),
        "search": bell_draw(key_list[1], (K, NX, NY * CZ), 0.5, 6.0, ((1, 32), (2, 16)), jnp.float32),
        "conductivity": jnp.clip(jnp.exp(math.log(5.0) - 3.218876 * jax.random.uniform(key_list[2], (NX, NY * CZ), jnp.float32) ** block_scale(key_list[2], (NX, NY * CZ), ((0, 32), (1, 16)), -0.2, 0.2)), 0.2, 5.0),
        "rotation": with_ends(jax.random.randint(key_list[3], (3 * K, K), -4, 5), jax.random.fold_in(key_list[3], 1), -4, 4).astype(jnp.int32),
    }


HIGH = lax.Precision.HIGHEST

def stencil(padded, cond_pad):
    middle = padded[:, 1:-1, 1:-1]
    cond_mid = cond_pad[1:-1, 1:-1]
    rows_x = middle.shape[1]
    rows_y = middle.shape[2]
    total = jnp.zeros_like(middle)
    for offset_x, offset_y in ((2, 1), (0, 1), (1, 2), (1, 0)):
        beside = padded[:, offset_x:offset_x + rows_x, offset_y:offset_y + rows_y]
        cond_side = cond_pad[offset_x:offset_x + rows_x, offset_y:offset_y + rows_y]
        total = total + 0.5 * (cond_mid + cond_side) * (middle - beside)
    for step_z in (1, -1):
        cond_side = jnp.roll(cond_mid, step_z, axis=2)
        total = total + 0.5 * (cond_mid + cond_side) * (middle - jnp.roll(middle, step_z, axis=3))
    return total

def cross(left, right):
    return lax.dot_general(left, right, (((1,), (1,)), ((), ())), precision=HIGH, preferred_element_type=jnp.float32)

def chol_lower(matrix):
    size = matrix.shape[0]
    index = lax.broadcasted_iota(jnp.int32, (size,), 0)

    def column(j, lower):
        row_j = lax.dynamic_slice_in_dim(lower, j, 1, 0)[0]
        col_a = lax.dynamic_slice_in_dim(matrix, j, 1, 1)[:, 0]
        vec = col_a - jnp.dot(lower, row_j, precision=HIGH)
        pivot = jnp.sqrt(jnp.sum(jnp.where(index == j, vec, 0.0)))
        col = jnp.where(index >= j, vec / pivot, 0.0)
        return jnp.where(index[None, :] == j, col[:, None], lower)
    return lax.fori_loop(0, size, column, jnp.zeros_like(matrix))

def lower_inverse(lower):
    size = lower.shape[0]
    index = lax.broadcasted_iota(jnp.int32, (size,), 0)
    ident = jnp.eye(size, dtype=lower.dtype)

    def row(i, result):
        l_row = lax.dynamic_slice_in_dim(lower, i, 1, 0)[0]
        e_row = lax.dynamic_slice_in_dim(ident, i, 1, 0)[0]
        pivot = jnp.sum(jnp.where(index == i, l_row, 0.0))
        fresh_row = (e_row - jnp.dot(l_row, result, precision=HIGH)) / pivot
        return jnp.where(index[:, None] == i, fresh_row[None, :], result)
    return lax.fori_loop(0, size, row, jnp.zeros_like(lower))

def finish(full, gram, projected, rotation):
    modes = rotation.shape[1]
    inverse = lower_inverse(chol_lower(gram)).T
    ritz = jnp.dot(inverse.T, jnp.dot(projected, inverse, precision=HIGH), precision=HIGH)
    ritz = 0.5 * (ritz + ritz.T)
    bound = jnp.max(lax.optimization_barrier(jnp.sum(jnp.abs(ritz), 1)))
    start = rotation.astype(gram.dtype)
    moved = bound * start - jnp.dot(ritz, start, precision=HIGH)
    lower = chol_lower(jnp.dot(moved.T, moved, precision=HIGH))
    coeffs = jnp.dot(moved, lower_inverse(lower).T, precision=HIGH)
    values = lax.optimization_barrier(jnp.sum(coeffs * jnp.dot(ritz, coeffs, precision=HIGH), 0))
    weights = jnp.dot(inverse, coeffs, precision=HIGH)
    dims = (((0,), (0,)), ((), ()))
    fresh = lax.dot_general(weights, full, dims, precision=HIGH, preferred_element_type=jnp.float32)
    directions = lax.dot_general(weights[modes:], full[modes:], dims, precision=HIGH, preferred_element_type=jnp.float32)
    return (fresh, directions, values)

def reference(basis, search, conductivity, rotation):
    modes, cells_x, flat = basis.shape
    cells_y = flat // CZ
    count = cells_x * flat
    cond_pad = jnp.pad(conductivity.reshape(cells_x, cells_y, CZ), ((1, 1), (1, 1), (0, 0)))

    def apply_op(field):
        padded = jnp.pad(field, ((0, 0), (1, 1), (1, 1), (0, 0)))
        return stencil(padded, cond_pad).reshape(field.shape[0], count)
    basis_flat = basis.reshape(modes, count)
    search_flat = search.reshape(modes, count)
    images = apply_op(jnp.concatenate([basis, search], 0).reshape(2 * modes, cells_x, cells_y, CZ))
    image_x = images[:modes]
    image_p = images[modes:]
    quotient = lax.optimization_barrier(jnp.sum(basis_flat * image_x, 1)) / lax.optimization_barrier(jnp.sum(basis_flat * basis_flat, 1))
    residual = image_x - quotient[:, None] * basis_flat
    image_w = apply_op(residual.reshape(modes, cells_x, cells_y, CZ))
    full = jnp.concatenate([basis_flat, residual, search_flat], 0)
    image_all = jnp.concatenate([image_x, image_w, image_p], 0)
    gram = cross(full, full) / count
    projected = cross(full, image_all) / count
    fresh, directions, values = finish(full, gram, projected, rotation)
    return (fresh.reshape(modes, cells_x, flat), directions.reshape(modes, cells_x, flat), values)
```

```python
import jax
import jax.numpy as jnp
import numpy as np
from jax import lax
from jax.experimental import pallas as pl
from jax.experimental.pallas import tpu as pltpu
from jax.sharding import PartitionSpec as P

CZ = 16
MODES = 32
ROWS = 8
LANES = 128
HIGH = lax.Precision.HIGHEST
VMEM = pl.BlockSpec(memory_space=pltpu.VMEM)


def dot_nt(left, right):
    return lax.dot_general(
        left, right, (((1,), (1,)), ((), ())), precision=HIGH, preferred_element_type=jnp.float32
    )


def dot_nn(left, right):
    return lax.dot_general(
        left, right, (((1,), (0,)), ((), ())), precision=HIGH, preferred_element_type=jnp.float32
    )


def roll(array, shift):
    shift = shift % LANES
    return pltpu.roll(array, shift, array.ndim - 1) if shift else array


def lanes(shape):
    return lax.broadcasted_iota(jnp.int32, shape, len(shape) - 1)


def pack_rows(basis_hbm, search_hbm, cond_hbm, up, down, basis, search, cond, arrived):
    copies = [
        pltpu.make_async_copy(source, target, arrived.at[k])
        for k, (source, target) in enumerate(
            ((basis_hbm, basis), (search_hbm, search), (cond_hbm, cond))
        )
    ]
    for copy in copies:
        copy.start()
    for copy in copies:
        copy.wait()
    for message, first, second, edge in ((up, 6, 7, 7), (down, 0, 1, 0)):
        message[0:32, :] = basis[:, first, :]
        message[32:64, :] = basis[:, second, :]
        message[64:96, :] = search[:, edge, :]
        message[96:104, :] = cond[...]


def pack_sides(basis, search, cond, lo, hi, right, left):
    fields = [lo[32:64, :]] + [basis[:, s, :] for s in range(ROWS)] + [hi[0:32, :]]
    fields += [search[:, s, :] for s in range(ROWS)]
    conds = [lo[103:104, :]] + [cond[s : s + 1, :] for s in range(ROWS)] + [hi[96:97, :]]
    for message, base in ((right, 32), (left, 0)):
        for rows, start, step in ((fields, 0, 32), (conds, 160, 1)):
            for tile in range((len(rows) + 3) // 4):
                packed = None
                for k, row in enumerate(rows[4 * tile : 4 * tile + 4]):
                    if step == 1:
                        row = jnp.broadcast_to(row, (8, LANES))
                    moved = roll(row, base + 32 * k)
                    if packed is None:
                        packed = moved
                    else:
                        packed = jnp.where(lanes(moved.shape) >= 32 * k, moved, packed)
                message[start + step * tile : start + step * (tile + 1), :] = packed[:step]
        message[163:168, :] = jnp.zeros((5, LANES), jnp.float32)


def side_tile(low, high, index, start, step):
    tile, k = divmod(index, 4)
    place = start + step * tile
    below = low[place : place + step, :]
    above = high[place : place + step, :]
    if step == 1:
        below = jnp.broadcast_to(below, (8, LANES))
        above = jnp.broadcast_to(above, (8, LANES))
    lane = lanes(below.shape)
    below = roll(below, 96 - 32 * k)
    above = roll(above, -32 * k)
    return jnp.where(lane >= 96, below, jnp.where(lane < 32, above, 0.0))


def next_y(own, side):
    lane = lanes(own.shape)
    a, b = roll(own, -CZ), roll(side, -CZ)
    return jnp.where(lane < LANES - CZ, a, b), jnp.where(lane < LANES - CZ, b, a)


def prev_y(own, side):
    lane = lanes(own.shape)
    a, b = roll(own, CZ), roll(side, CZ)
    return jnp.where(lane >= CZ, a, b), jnp.where(lane >= CZ, b, a)


def next_z(array):
    return jnp.where(lanes(array.shape) % CZ == CZ - 1, roll(array, CZ - 1), roll(array, -1))


def prev_z(array):
    return jnp.where(lanes(array.shape) % CZ == 0, roll(array, 1 - CZ), roll(array, 1))


def images(basis, search, cond, lo, hi, low, high, fields, sums, conds, coef, image, stack):
    conds[...] = jnp.zeros_like(conds)
    conds[0, 0:2, :] = lo[102:104, :]
    conds[0, 2:10, :] = cond[...]
    conds[0, 10:12, :] = hi[96:98, :]
    for r in range(10):
        conds[1, r + 1 : r + 2, :] = side_tile(low, high, r, 160, 1)[:1]
    cond_a, cond_b = conds[0, 0:16, :], conds[1, 0:16, :]
    after = next_y(cond_a, cond_b)
    before = prev_y(cond_a, cond_b)
    for part, array in ((0, cond_a), (1, cond_b)):
        coef[part, 0] = 0.5 * (array + conds[part, 1:17, :])
        coef[part, 1] = 0.5 * (array + after[part])
        coef[part, 2] = 0.5 * (array + before[part])
        coef[part, 3] = 0.5 * (array + next_z(array))
        coef[part, 4] = 0.5 * (array + prev_z(array))

    def operator(part, r, own, beside, x_low, x_high):
        i = r + 2
        total = coef[part, 0, i - 1 : i, :] * (own - x_low)
        total += coef[part, 0, i : i + 1, :] * (own - x_high)
        total += coef[part, 1, i : i + 1, :] * (own - beside[0])
        total += coef[part, 2, i : i + 1, :] * (own - beside[1])
        total += coef[part, 3, i : i + 1, :] * (own - next_z(own))
        total += coef[part, 4, i : i + 1, :] * (own - prev_z(own))
        return total

    def beside(own, side):
        after, before = next_y(own, side), prev_y(own, side)
        return ((after[0], before[0]), (after[1], before[1]))

    def basis_row(r):
        if r < 0:
            return lo[32 * (r + 2) : 32 * (r + 3), :]
        if r >= ROWS:
            return hi[32 * (r - ROWS) : 32 * (r - ROWS + 1), :]
        return basis[:, r, :]

    def valid(part, r, array):
        return jnp.where(conds[part, r + 2 : r + 3, :] > 0.0, array, 0.0)

    sides = {r: side_tile(low, high, r + 1, 0, 32) for r in range(-1, 2)}
    for r in range(-1, ROWS + 1):
        if 1 <= r < ROWS:
            sides[r + 1] = side_tile(low, high, r + 2, 0, 32)
        own = basis_row(r)
        pairs = beside(own, sides[r])
        first = operator(0, r, own, pairs[0], basis_row(r - 1), basis_row(r + 1))
        image[0, r + 1] = first if 0 <= r < ROWS else valid(0, r, first)
        if 0 <= r < ROWS:
            second = operator(1, r, sides[r], pairs[1], sides[r - 1], sides[r + 1])
            image[1, r + 1] = valid(1, r, second)

    for s in range(ROWS):
        at = slice(LANES * s, LANES * (s + 1))
        field = search[:, s, :]
        pairs = beside(field, side_tile(low, high, 10 + s, 0, 32))
        x_low = lo[64:96, :] if s == 0 else search[:, s - 1, :]
        x_high = hi[64:96, :] if s == ROWS - 1 else search[:, s + 1, :]
        stack[128:160, at] = operator(0, s, field, pairs[0], x_low, x_high)
        own = image[0, s + 1]
        pairs = beside(own, image[1, s + 1])
        stack[96:128, at] = operator(0, s, own, pairs[0], image[0, s], image[0, s + 2])
        stack[0:32, at] = basis[:, s, :]
        stack[32:64, at] = own
        stack[64:96, at] = field
        fields[0:32, at] = basis[:, s, :]
        fields[32:64, at] = own
        fields[64:96, at] = field

    product = dot_nt(stack[0:96, :], stack[...])
    last = product[64:96, 128:160]
    sums[0:32, :] = jnp.concatenate([product[0:32, 0:96], last], 1)
    sums[32:64, :] = jnp.concatenate([product[64:96, 96:128], product[32:64, 32:128]], 1)
    corner = product[64:96, 64:96]
    sums[64:72, :] = jnp.concatenate([corner[8 * k : 8 * k + 8] for k in range(4)], 1)
    sums[72:128, :] = jnp.zeros((56, LANES), jnp.float32)


def eliminate(slabs):
    slabs = list(slabs)
    count = len(slabs)
    lane = lanes((8, LANES))
    row = lax.broadcasted_iota(jnp.int32, (8, LANES), 0)
    width = 4
    for start in range(0, 8 * count, width):
        g = start // 8
        cols = [
            {i: jnp.broadcast_to(slabs[i][:, start + k : start + k + 1], (8, LANES)) for i in range(g, count)}
            for k in range(width)
        ]
        for k in range(width):
            j = start + k
            at = j % 8
            pivot = cols[k][g][at : at + 1, :]
            inverse = 1.0 / pivot
            root = lax.rsqrt(pivot)
            here = lane[:1] == j
            pivot_row = jnp.where(here, 1.0, slabs[g][at : at + 1, :])
            scaled = pivot_row * inverse
            later = [cols[m][g][at : at + 1, :] * inverse for m in range(k + 1, width)]
            for i in range(g, count):
                factor = cols[k][i]
                kept = jnp.where(lane == j, 0.0, slabs[i])
                if i == g:
                    factor = jnp.where(row > at, factor, 0.0)
                    kept = jnp.where(row > at, kept, slabs[i])
                    fresh = kept - factor * scaled
                    slabs[i] = jnp.where(row == at, pivot_row * root, fresh)
                else:
                    slabs[i] = kept - factor * scaled
                for m in range(k + 1, width):
                    cols[m][i] = cols[m][i] - factor * later[m - k - 1]
    return slabs


def lower_part(slabs, size):
    whole = jnp.concatenate(slabs, 0)
    row = lax.broadcasted_iota(jnp.int32, whole.shape, 0)
    return jnp.where(lanes(whole.shape) <= row, whole, 0.0)[:, :size]


def update(scale, sums, start, fields, new_basis, new_search, values):
    first = sums[0:32, :] * scale
    second = sums[32:64, :] * scale
    third = sums[64:72, :] * scale
    xx, xy, xp, pr = (first[:, 32 * k : 32 * k + 32] for k in range(4))
    pz, yy, yp, yz = (second[:, 32 * k : 32 * k + 32] for k in range(4))
    pp = jnp.concatenate([third[:, 32 * k : 32 * k + 32] for k in range(4)], 0)
    px, py, zp = xp.T, yp.T, pz.T
    zero = jnp.zeros((32, 32), jnp.float32)
    gram = [
        jnp.concatenate([xx, xy, xp, zero], 1),
        jnp.concatenate([xy, yy, yp, zero], 1),
        jnp.concatenate([px, py, pp, zero], 1),
    ]
    projected = jnp.concatenate(
        [
            jnp.concatenate([xy, yy, yp], 1),
            jnp.concatenate([yy, yz, zp], 1),
            jnp.concatenate([py, pz, pr], 1),
        ],
        0,
    )
    lower_inv = lower_part(
        eliminate([block[8 * k : 8 * k + 8] for block in gram for k in range(4)]), 96
    )
    ritz = dot_nt(dot_nn(lower_inv, projected), lower_inv)
    ritz = 0.5 * (ritz + ritz.T)
    bound = jnp.max(jnp.sum(jnp.abs(ritz), 0, keepdims=True), 1, keepdims=True)
    seed = start[...].astype(jnp.float32)
    moved = bound * seed - dot_nn(seed, ritz)
    square = jnp.concatenate([dot_nt(moved, moved), jnp.zeros((32, 96), jnp.float32)], 1)
    small_inv = lower_part(eliminate([square[8 * k : 8 * k + 8] for k in range(4)]), 32)
    coeffs = dot_nn(small_inv, moved)
    weights = dot_nn(coeffs, lower_inv)
    terms = coeffs * dot_nn(coeffs, ritz)
    values[...] = dot_nt(jnp.ones((8, 96), jnp.float32), terms)[0:1, :]
    diagonal = lanes((32, 32)) == lax.broadcasted_iota(jnp.int32, (32, 32), 0)
    along = jnp.sum(jnp.where(diagonal, xy, 0.0), 0, keepdims=True)
    norms = jnp.sum(jnp.where(diagonal, xx, 0.0), 0, keepdims=True)
    quotient = along / norms
    middle = weights[:, 32:64]
    search_weights = jnp.concatenate([-(middle * quotient), middle, weights[:, 64:96]], 1)
    both = jnp.concatenate([weights, search_weights], 0)
    result = dot_nn(both, fields[...])
    for s in range(ROWS):
        new_basis[:, s, :] = result[0:32, LANES * s : LANES * (s + 1)]
        new_search[:, s, :] = result[32:64, LANES * s : LANES * (s + 1)]


def call(kernel, outs, *args, scratch=(), place=VMEM, room=32):
    shapes = [jax.ShapeDtypeStruct(shape, jnp.float32) for shape in outs]
    return pl.pallas_call(
        kernel,
        out_shape=shapes,
        in_specs=[place] * len(args),
        out_specs=[VMEM] * len(shapes),
        scratch_shapes=[
            pltpu.VMEM(shape, jnp.float32) if isinstance(shape, tuple) else shape for shape in scratch
        ],
        compiler_params=pltpu.CompilerParams(vmem_limit_bytes=room * 1024 * 1024),
    )(*args)


def shifted(array, axis, step):
    count = lax.axis_size(axis)
    return lax.ppermute(array, axis, [(i, i + step) for i in range(count) if 0 <= i + step < count])


def summed(array, count):
    return jnp.sum(array.reshape(count, array.shape[0] // count, LANES), 0)


def groups(sizes, free):
    index = np.arange(int(np.prod(sizes))).reshape(sizes)
    kept = [axis for axis in range(len(sizes)) if axis not in free]
    count = int(np.prod([sizes[axis] for axis in free]))
    return index.transpose(kept + list(free)).reshape(-1, count).tolist()


def total(array):
    along, across = lax.axis_size("gx"), lax.axis_size("gy")
    sizes = (along // 4, 4, across // 2, 2)

    def exchanged(parts, free):
        return lax.all_to_all(
            parts, ("gx", "gy"), 0, 0, axis_index_groups=groups(sizes, free), tiled=True
        )

    share = summed(exchanged(array, (1, 3)), 8)
    for axis in (2, 0):
        share = summed(exchanged(jnp.tile(share, (sizes[axis], 1)), (axis,)), sizes[axis])
    return exchanged(jnp.tile(share, (8, 1)), (1, 3))


def body(basis, search, conductivity, rotation):
    modes, cells_x, flat = basis.shape
    count = cells_x * flat * lax.axis_size("gx") * lax.axis_size("gy")
    blocks = [basis.shape, search.shape, conductivity.shape]
    up, down = call(
        pack_rows,
        [(104, LANES)] * 2,
        basis,
        search,
        conductivity,
        scratch=blocks + [pltpu.SemaphoreType.DMA((3,))],
        place=pl.BlockSpec(memory_space=pl.ANY),
        room=63,
    )
    lo, hi = shifted(up, "gx", 1), shifted(down, "gx", -1)
    right, left = call(pack_sides, [(168, LANES)] * 2, basis, search, conductivity, lo, hi)
    low, high = shifted(right, "gy", 1), shifted(left, "gy", -1)
    fields, sums = call(
        images,
        [(96, ROWS * LANES), (LANES, LANES)],
        basis,
        search,
        conductivity,
        lo,
        hi,
        low,
        high,
        scratch=[(2, 24, LANES), (2, 5, 16, LANES), (2, 10, MODES, LANES), (160, ROWS * LANES)],
    )
    sums = total(sums)

    def finish(*refs):
        update(1.0 / count, *refs)

    new_basis, new_search, values = call(
        finish,
        [(modes, cells_x, flat), (modes, cells_x, flat), (1, modes)],
        sums,
        rotation.T,
        fields,
    )
    return new_basis, new_search, values.reshape(modes)


def solution(mesh):
    in_specs = (P(None, "gx", "gy"), P(None, "gx", "gy"), P("gx", "gy"), P())
    out_specs = (P(None, "gx", "gy"), P(None, "gx", "gy"), P())
    return jax.shard_map(body, mesh=mesh, in_specs=in_specs, out_specs=out_specs, check_vma=False)
```

```python
import jax
import jax.numpy as jnp
from jax import lax
from jax.experimental import pallas as pl
from jax.experimental.pallas import tpu as pltpu
from jax.sharding import PartitionSpec as P

CZ = 16
MODES = 32
ROWS = 8
LANES = 128
HIGH = lax.Precision.HIGHEST
VMEM = pl.BlockSpec(memory_space=pltpu.VMEM)


def dot_nt(left, right):
    return lax.dot_general(
        left, right, (((1,), (1,)), ((), ())), precision=HIGH, preferred_element_type=jnp.float32
    )


def dot_nn(left, right):
    return lax.dot_general(
        left, right, (((1,), (0,)), ((), ())), precision=HIGH, preferred_element_type=jnp.float32
    )


def roll(array, shift):
    shift = shift % LANES
    return pltpu.roll(array, shift, array.ndim - 1) if shift else array


def lanes(shape):
    return lax.broadcasted_iota(jnp.int32, shape, len(shape) - 1)


def is_odd(axis):
    return lax.axis_index(axis) % 2 == 1


def sort_sides(axis, one, two, low, high):
    odd = is_odd(axis)
    low[...] = jnp.where(odd, one[...], two[...])
    high[...] = jnp.where(odd, two[...], one[...])


def pack_rows(basis_hbm, search_hbm, cond_hbm, one, two, basis, search, cond, arrived):
    copies = [
        pltpu.make_async_copy(source, target, arrived.at[k])
        for k, (source, target) in enumerate(
            ((basis_hbm, basis), (search_hbm, search), (cond_hbm, cond))
        )
    ]
    for copy in copies:
        copy.start()
    for copy in copies:
        copy.wait()
    up = [basis[:, 6, :], basis[:, 7, :], search[:, 7, :]]
    down = [basis[:, 0, :], basis[:, 1, :], search[:, 0, :]]
    odd = is_odd("gx")
    for k in range(3):
        one[32 * k : 32 * k + 32, :] = jnp.where(odd, down[k], up[k])
        two[32 * k : 32 * k + 32, :] = jnp.where(odd, up[k], down[k])
    one[96:104, :] = cond[...]
    two[96:104, :] = cond[...]


def pack_sides(basis, search, cond, row_one, row_two, side_one, side_two, lo, hi, right, left):
    sort_sides("gx", row_one, row_two, lo, hi)
    fields = [lo[32:64, :]] + [basis[:, s, :] for s in range(ROWS)] + [hi[0:32, :]]
    fields += [search[:, s, :] for s in range(ROWS)]
    conds = [lo[103:104, :]] + [cond[s : s + 1, :] for s in range(ROWS)] + [hi[96:97, :]]
    for message, base in ((right, 32), (left, 0)):
        for rows, start, step in ((fields, 0, 32), (conds, 160, 1)):
            for tile in range((len(rows) + 3) // 4):
                packed = None
                for k, row in enumerate(rows[4 * tile : 4 * tile + 4]):
                    if step == 1:
                        row = jnp.broadcast_to(row, (8, LANES))
                    moved = roll(row, base + 32 * k)
                    if packed is None:
                        packed = moved
                    else:
                        packed = jnp.where(lanes(moved.shape) >= 32 * k, moved, packed)
                message[start + step * tile : start + step * (tile + 1), :] = packed[:step]
        message[163:168, :] = jnp.zeros((5, LANES), jnp.float32)
    sort_sides("gy", left, right, side_one, side_two)


def side_tile(low, high, index, start, step):
    tile, k = divmod(index, 4)
    place = start + step * tile
    below = low[place : place + step, :]
    above = high[place : place + step, :]
    if step == 1:
        below = jnp.broadcast_to(below, (8, LANES))
        above = jnp.broadcast_to(above, (8, LANES))
    lane = lanes(below.shape)
    below = roll(below, 96 - 32 * k)
    above = roll(above, -32 * k)
    return jnp.where(lane >= 96, below, jnp.where(lane < 32, above, 0.0))


def next_y(own, side):
    lane = lanes(own.shape)
    a, b = roll(own, -CZ), roll(side, -CZ)
    return jnp.where(lane < LANES - CZ, a, b), jnp.where(lane < LANES - CZ, b, a)


def prev_y(own, side):
    lane = lanes(own.shape)
    a, b = roll(own, CZ), roll(side, CZ)
    return jnp.where(lane >= CZ, a, b), jnp.where(lane >= CZ, b, a)


def next_z(array):
    return jnp.where(lanes(array.shape) % CZ == CZ - 1, roll(array, CZ - 1), roll(array, -1))


def prev_z(array):
    return jnp.where(lanes(array.shape) % CZ == 0, roll(array, 1 - CZ), roll(array, 1))


def images(
    basis, search, cond, lo, hi, side_one, side_two, fields, sums, conds, coef, image, stack, low, high
):
    sort_sides("gy", side_one, side_two, low, high)
    conds[...] = jnp.zeros_like(conds)
    conds[0, 0:2, :] = lo[102:104, :]
    conds[0, 2:10, :] = cond[...]
    conds[0, 10:12, :] = hi[96:98, :]
    for r in range(10):
        conds[1, r + 1 : r + 2, :] = side_tile(low, high, r, 160, 1)[:1]
    cond_a, cond_b = conds[0, 0:16, :], conds[1, 0:16, :]
    after = next_y(cond_a, cond_b)
    before = prev_y(cond_a, cond_b)
    for part, array in ((0, cond_a), (1, cond_b)):
        coef[part, 0] = 0.5 * (array + conds[part, 1:17, :])
        coef[part, 1] = 0.5 * (array + after[part])
        coef[part, 2] = 0.5 * (array + before[part])
        coef[part, 3] = 0.5 * (array + next_z(array))
        coef[part, 4] = 0.5 * (array + prev_z(array))

    def operator(part, r, own, beside, x_low, x_high):
        i = r + 2
        total = coef[part, 0, i - 1 : i, :] * (own - x_low)
        total += coef[part, 0, i : i + 1, :] * (own - x_high)
        total += coef[part, 1, i : i + 1, :] * (own - beside[0])
        total += coef[part, 2, i : i + 1, :] * (own - beside[1])
        total += coef[part, 3, i : i + 1, :] * (own - next_z(own))
        total += coef[part, 4, i : i + 1, :] * (own - prev_z(own))
        return total

    def beside(own, side):
        after, before = next_y(own, side), prev_y(own, side)
        return ((after[0], before[0]), (after[1], before[1]))

    def basis_row(r):
        if r < 0:
            return lo[32 * (r + 2) : 32 * (r + 3), :]
        if r >= ROWS:
            return hi[32 * (r - ROWS) : 32 * (r - ROWS + 1), :]
        return basis[:, r, :]

    def valid(part, r, array):
        return jnp.where(conds[part, r + 2 : r + 3, :] > 0.0, array, 0.0)

    sides = {r: side_tile(low, high, r + 1, 0, 32) for r in range(-1, 2)}
    for r in range(-1, ROWS + 1):
        if 1 <= r < ROWS:
            sides[r + 1] = side_tile(low, high, r + 2, 0, 32)
        own = basis_row(r)
        pairs = beside(own, sides[r])
        first = operator(0, r, own, pairs[0], basis_row(r - 1), basis_row(r + 1))
        image[0, r + 1] = first if 0 <= r < ROWS else valid(0, r, first)
        if 0 <= r < ROWS:
            second = operator(1, r, sides[r], pairs[1], sides[r - 1], sides[r + 1])
            image[1, r + 1] = valid(1, r, second)

    for s in range(ROWS):
        at = slice(LANES * s, LANES * (s + 1))
        field = search[:, s, :]
        pairs = beside(field, side_tile(low, high, 10 + s, 0, 32))
        x_low = lo[64:96, :] if s == 0 else search[:, s - 1, :]
        x_high = hi[64:96, :] if s == ROWS - 1 else search[:, s + 1, :]
        stack[128:160, at] = operator(0, s, field, pairs[0], x_low, x_high)
        own = image[0, s + 1]
        pairs = beside(own, image[1, s + 1])
        stack[96:128, at] = operator(0, s, own, pairs[0], image[0, s], image[0, s + 2])
        stack[0:32, at] = basis[:, s, :]
        stack[32:64, at] = own
        stack[64:96, at] = field
        fields[0:32, at] = basis[:, s, :]
        fields[32:64, at] = own
        fields[64:96, at] = field

    product = dot_nt(stack[0:96, :], stack[...])
    last = product[64:96, 128:160]
    sums[0:32, :] = jnp.concatenate([product[0:32, 0:96], last], 1)
    sums[32:64, :] = jnp.concatenate([product[64:96, 96:128], product[32:64, 32:128]], 1)
    corner = product[64:96, 64:96]
    sums[64:72, :] = jnp.concatenate([corner[8 * k : 8 * k + 8] for k in range(4)], 1)
    sums[72:128, :] = jnp.zeros((56, LANES), jnp.float32)


def eliminate(slabs):
    slabs = list(slabs)
    count = len(slabs)
    lane = lanes((8, LANES))
    row = lax.broadcasted_iota(jnp.int32, (8, LANES), 0)
    width = 4
    for start in range(0, 8 * count, width):
        g = start // 8
        cols = [
            {i: jnp.broadcast_to(slabs[i][:, start + k : start + k + 1], (8, LANES)) for i in range(g, count)}
            for k in range(width)
        ]
        for k in range(width):
            j = start + k
            at = j % 8
            pivot = cols[k][g][at : at + 1, :]
            inverse = 1.0 / pivot
            root = lax.rsqrt(pivot)
            here = lane[:1] == j
            pivot_row = jnp.where(here, 1.0, slabs[g][at : at + 1, :])
            scaled = pivot_row * inverse
            later = [cols[m][g][at : at + 1, :] * inverse for m in range(k + 1, width)]
            for i in range(g, count):
                factor = cols[k][i]
                kept = jnp.where(lane == j, 0.0, slabs[i])
                if i == g:
                    factor = jnp.where(row > at, factor, 0.0)
                    kept = jnp.where(row > at, kept, slabs[i])
                    fresh = kept - factor * scaled
                    slabs[i] = jnp.where(row == at, pivot_row * root, fresh)
                else:
                    slabs[i] = kept - factor * scaled
                for m in range(k + 1, width):
                    cols[m][i] = cols[m][i] - factor * later[m - k - 1]
    return slabs


def lower_part(slabs, size):
    whole = jnp.concatenate(slabs, 0)
    row = lax.broadcasted_iota(jnp.int32, whole.shape, 0)
    return jnp.where(lanes(whole.shape) <= row, whole, 0.0)[:, :size]


def update(scale, sums, start, fields, new_basis, new_search, values):
    first = sums[0:32, :] * scale
    second = sums[32:64, :] * scale
    third = sums[64:72, :] * scale
    xx, xy, xp, pr = (first[:, 32 * k : 32 * k + 32] for k in range(4))
    pz, yy, yp, yz = (second[:, 32 * k : 32 * k + 32] for k in range(4))
    pp = jnp.concatenate([third[:, 32 * k : 32 * k + 32] for k in range(4)], 0)
    px, py, zp = xp.T, yp.T, pz.T
    zero = jnp.zeros((32, 32), jnp.float32)
    gram = [
        jnp.concatenate([xx, xy, xp, zero], 1),
        jnp.concatenate([xy, yy, yp, zero], 1),
        jnp.concatenate([px, py, pp, zero], 1),
    ]
    projected = jnp.concatenate(
        [
            jnp.concatenate([xy, yy, yp], 1),
            jnp.concatenate([yy, yz, zp], 1),
            jnp.concatenate([py, pz, pr], 1),
        ],
        0,
    )
    lower_inv = lower_part(
        eliminate([block[8 * k : 8 * k + 8] for block in gram for k in range(4)]), 96
    )
    ritz = dot_nt(dot_nn(lower_inv, projected), lower_inv)
    ritz = 0.5 * (ritz + ritz.T)
    bound = jnp.max(jnp.sum(jnp.abs(ritz), 0, keepdims=True), 1, keepdims=True)
    seed = start[...].astype(jnp.float32)
    moved = bound * seed - dot_nn(seed, ritz)
    square = jnp.concatenate([dot_nt(moved, moved), jnp.zeros((32, 96), jnp.float32)], 1)
    small_inv = lower_part(eliminate([square[8 * k : 8 * k + 8] for k in range(4)]), 32)
    coeffs = dot_nn(small_inv, moved)
    weights = dot_nn(coeffs, lower_inv)
    terms = coeffs * dot_nn(coeffs, ritz)
    values[...] = dot_nt(jnp.ones((8, 96), jnp.float32), terms)[0:1, :]
    diagonal = lanes((32, 32)) == lax.broadcasted_iota(jnp.int32, (32, 32), 0)
    along = jnp.sum(jnp.where(diagonal, xy, 0.0), 0, keepdims=True)
    norms = jnp.sum(jnp.where(diagonal, xx, 0.0), 0, keepdims=True)
    quotient = along / norms
    middle = weights[:, 32:64]
    search_weights = jnp.concatenate([-(middle * quotient), middle, weights[:, 64:96]], 1)
    both = jnp.concatenate([weights, search_weights], 0)
    result = dot_nn(both, fields[...])
    for s in range(ROWS):
        new_basis[:, s, :] = result[0:32, LANES * s : LANES * (s + 1)]
        new_search[:, s, :] = result[32:64, LANES * s : LANES * (s + 1)]


def call(kernel, outs, *args, scratch=(), place=VMEM, room=32):
    shapes = [jax.ShapeDtypeStruct(shape, jnp.float32) for shape in outs]
    return pl.pallas_call(
        kernel,
        out_shape=shapes,
        in_specs=[place] * len(args),
        out_specs=[VMEM] * len(shapes),
        scratch_shapes=[
            pltpu.VMEM(shape, jnp.float32) if isinstance(shape, tuple) else shape for shape in scratch
        ],
        compiler_params=pltpu.CompilerParams(vmem_limit_bytes=room * 1024 * 1024),
    )(*args)


def paired(array, axis, first):
    pairs = [(i, i + 1) for i in range(first, lax.axis_size(axis) - 1, 2)]
    return lax.ppermute(array, axis, pairs + [(j, i) for i, j in pairs])


def exchanged(array, axis):
    return lax.all_to_all(array, axis, 0, 0, tiled=True)


def summed(array, count):
    return jnp.sum(array.reshape(count, array.shape[0] // count, LANES), 0)


def total(array):
    across, along = lax.axis_size("gy"), lax.axis_size("gx")
    share = summed(exchanged(array, "gy"), across)
    share = summed(exchanged(jnp.tile(share, (along, 1)), "gx"), along)
    return exchanged(jnp.tile(share, (across, 1)), "gy")


def body(basis, search, conductivity, rotation):
    modes, cells_x, flat = basis.shape
    count = cells_x * flat * lax.axis_size("gx") * lax.axis_size("gy")
    blocks = [basis.shape, search.shape, conductivity.shape]
    rows = call(
        pack_rows,
        [(104, LANES)] * 2,
        basis,
        search,
        conductivity,
        scratch=blocks + [pltpu.SemaphoreType.DMA((3,))],
        place=pl.BlockSpec(memory_space=pl.ANY),
        room=63,
    )
    rows = [paired(rows[k], "gx", k) for k in range(2)]
    side_one, side_two, lo, hi = call(
        pack_sides,
        [(168, LANES)] * 2 + [(104, LANES)] * 2,
        basis,
        search,
        conductivity,
        *rows,
        scratch=[(168, LANES)] * 2,
    )
    side_one, side_two = paired(side_one, "gy", 0), paired(side_two, "gy", 1)
    fields, sums = call(
        images,
        [(96, ROWS * LANES), (LANES, LANES)],
        basis,
        search,
        conductivity,
        lo,
        hi,
        side_one,
        side_two,
        scratch=[(2, 24, LANES), (2, 5, 16, LANES), (2, 10, MODES, LANES), (160, ROWS * LANES)]
        + [(168, LANES)] * 2,
    )
    sums = total(sums)

    def finish(*refs):
        update(1.0 / count, *refs)

    new_basis, new_search, values = call(
        finish,
        [(modes, cells_x, flat), (modes, cells_x, flat), (1, modes)],
        sums,
        rotation.T,
        fields,
    )
    return new_basis, new_search, values.reshape(modes)


def solution(mesh):
    in_specs = (P(None, "gx", "gy"), P(None, "gx", "gy"), P("gx", "gy"), P())
    out_specs = (P(None, "gx", "gy"), P(None, "gx", "gy"), P())
    return jax.shard_map(body, mesh=mesh, in_specs=in_specs, out_specs=out_specs, check_vma=False)
```

```python
import jax
import jax.numpy as jnp
from jax import lax
from jax.experimental import pallas as pl
from jax.experimental.pallas import tpu as pltpu
from jax.sharding import PartitionSpec as P

CZ = 16
MODES = 32
ROWS = 8
LANES = 128
HIGH = lax.Precision.HIGHEST
VMEM = pl.BlockSpec(memory_space=pltpu.VMEM)


def dot_nt(left, right):
    return lax.dot_general(
        left, right, (((1,), (1,)), ((), ())), precision=HIGH, preferred_element_type=jnp.float32
    )


def dot_nn(left, right):
    return lax.dot_general(
        left, right, (((1,), (0,)), ((), ())), precision=HIGH, preferred_element_type=jnp.float32
    )


def roll(array, shift):
    shift = shift % LANES
    return pltpu.roll(array, shift, array.ndim - 1) if shift else array


def lanes(shape):
    return lax.broadcasted_iota(jnp.int32, shape, len(shape) - 1)


def is_odd(axis):
    return lax.axis_index(axis) % 2 == 1


def sort_sides(axis, one, two, low, high):
    odd = is_odd(axis)
    low[...] = jnp.where(odd, one[...], two[...])
    high[...] = jnp.where(odd, two[...], one[...])


def pack_rows(basis_hbm, search_hbm, cond_hbm, one, two, basis, search, cond, arrived):
    copies = [
        pltpu.make_async_copy(source, target, arrived.at[k])
        for k, (source, target) in enumerate(
            ((basis_hbm, basis), (search_hbm, search), (cond_hbm, cond))
        )
    ]
    for copy in copies:
        copy.start()
    for copy in copies:
        copy.wait()
    up = [basis[:, 6, :], basis[:, 7, :], search[:, 7, :]]
    down = [basis[:, 0, :], basis[:, 1, :], search[:, 0, :]]
    odd = is_odd("gx")
    for k in range(3):
        one[32 * k : 32 * k + 32, :] = jnp.where(odd, down[k], up[k])
        two[32 * k : 32 * k + 32, :] = jnp.where(odd, up[k], down[k])
    one[96:104, :] = cond[...]
    two[96:104, :] = cond[...]


def pack_layers(rows, right):
    lane = lanes(rows[0].shape) // CZ
    outer = second = None
    for s in range(ROWS):
        moved = roll(rows[s], CZ * (s + 1 if right else s))
        at = (s - 1 if right else s + 1) % ROWS
        outer = moved if outer is None else jnp.where(lane == s, moved, outer)
        second = moved if second is None else jnp.where(lane == at, moved, second)
    return outer, second


def pack_ends(before, after, right):
    before = roll(before, CZ if right else 0)
    after = roll(after, 2 * CZ if right else CZ)
    return jnp.where(lanes(before.shape) < CZ, before, after)


def pack_sides(basis, search, cond, row_two, row_one, side_one, side_two, lo, hi, right, left):
    sort_sides("gx", row_one, row_two, lo, hi)
    block = (8, LANES)
    field = [basis[:, s, :] for s in range(ROWS)]
    other = [search[:, s, :] for s in range(ROWS)]
    cells = [jnp.broadcast_to(cond[s : s + 1, :], block) for s in range(ROWS)]
    cell_lo = jnp.broadcast_to(lo[103:104, :], block)
    cell_hi = jnp.broadcast_to(hi[96:97, :], block)
    lane = lanes(block)
    for message, to_right in ((right, True), (left, False)):
        message[0:32, :], message[32:64, :] = pack_layers(field, to_right)
        message[64:96, :] = pack_layers(other, to_right)[0]
        ends = pack_ends(lo[32:64, :], hi[0:32, :], to_right)
        folded = ends[0:8]
        for q in range(1, 4):
            folded = jnp.where(lane >= 32 * q, roll(ends[8 * q : 8 * q + 8], 32 * q), folded)
        message[96:104, :] = folded
        cell_outer, cell_second = pack_layers(cells, to_right)
        message[104:105, :] = cell_outer[:1]
        message[105:106, :] = cell_second[:1]
        message[106:107, :] = pack_ends(cell_lo, cell_hi, to_right)[:1]
        message[107:112, :] = jnp.zeros((5, LANES), jnp.float32)
    sort_sides("gy", left, right, side_one, side_two)


def side_tile(low, high, s):
    lane = lanes(low[0].shape) // CZ
    if 0 <= s < ROWS:
        above = [roll(part, -CZ * s) for part in high[:2]]
        below = [roll(part, CZ * (7 - s)) for part in low[:2]]
        tile = jnp.where(lane == 0, above[0], jnp.where(lane == 7, below[0], 0.0))
        if len(above) == 2:
            tile = jnp.where(lane == 1, above[1], jnp.where(lane == 6, below[1], tile))
        return tile
    k = 0 if s < 0 else 1
    above, below = roll(high[2], -CZ * k), roll(low[2], CZ * (7 - k))
    return jnp.where(lane == 0, above, jnp.where(lane == 7, below, 0.0))


def unfolded(folded):
    return jnp.concatenate([roll(folded, -32 * q) for q in range(4)], 0)


def next_y(own, side):
    lane = lanes(own.shape)
    a, b = roll(own, -CZ), roll(side, -CZ)
    return jnp.where(lane < LANES - CZ, a, b), jnp.where(lane < LANES - CZ, b, a)


def prev_y(own, side):
    lane = lanes(own.shape)
    a, b = roll(own, CZ), roll(side, CZ)
    return jnp.where(lane >= CZ, a, b), jnp.where(lane >= CZ, b, a)


def next_z(array):
    return jnp.where(lanes(array.shape) % CZ == CZ - 1, roll(array, CZ - 1), roll(array, -1))


def prev_z(array):
    return jnp.where(lanes(array.shape) % CZ == 0, roll(array, 1 - CZ), roll(array, 1))


def images(
    basis, search, cond, lo, hi, side_two, side_one, fields, sums, conds, coef, image, stack, low, high
):
    sort_sides("gy", side_one, side_two, low, high)
    basis_sides = [(part[0:32, :], part[32:64, :], unfolded(part[96:104, :])) for part in (low, high)]
    search_sides = [(part[64:96, :],) for part in (low, high)]
    cond_sides = [
        [jnp.broadcast_to(part[r : r + 1, :], (8, LANES)) for r in range(104, 107)] for part in (low, high)
    ]
    conds[...] = jnp.zeros_like(conds)
    conds[0, 0:2, :] = lo[102:104, :]
    conds[0, 2:10, :] = cond[...]
    conds[0, 10:12, :] = hi[96:98, :]
    for r in range(10):
        conds[1, r + 1 : r + 2, :] = side_tile(*cond_sides, r - 1)[:1]
    cond_a, cond_b = conds[0, 0:16, :], conds[1, 0:16, :]
    after = next_y(cond_a, cond_b)
    before = prev_y(cond_a, cond_b)
    for part, array in ((0, cond_a), (1, cond_b)):
        coef[part, 0] = 0.5 * (array + conds[part, 1:17, :])
        coef[part, 1] = 0.5 * (array + after[part])
        coef[part, 2] = 0.5 * (array + before[part])
        coef[part, 3] = 0.5 * (array + next_z(array))
        coef[part, 4] = 0.5 * (array + prev_z(array))

    def operator(part, r, own, beside, x_low, x_high):
        i = r + 2
        total = coef[part, 0, i - 1 : i, :] * (own - x_low)
        total += coef[part, 0, i : i + 1, :] * (own - x_high)
        total += coef[part, 1, i : i + 1, :] * (own - beside[0])
        total += coef[part, 2, i : i + 1, :] * (own - beside[1])
        total += coef[part, 3, i : i + 1, :] * (own - next_z(own))
        total += coef[part, 4, i : i + 1, :] * (own - prev_z(own))
        return total

    def beside(own, side):
        after, before = next_y(own, side), prev_y(own, side)
        return ((after[0], before[0]), (after[1], before[1]))

    def basis_row(r):
        if r < 0:
            return lo[32 * (r + 2) : 32 * (r + 3), :]
        if r >= ROWS:
            return hi[32 * (r - ROWS) : 32 * (r - ROWS + 1), :]
        return basis[:, r, :]

    def valid(part, r, array):
        return jnp.where(conds[part, r + 2 : r + 3, :] > 0.0, array, 0.0)

    sides = {r: side_tile(*basis_sides, r) for r in range(-1, 2)}
    for r in range(-1, ROWS + 1):
        if 1 <= r < ROWS:
            sides[r + 1] = side_tile(*basis_sides, r + 1)
        own = basis_row(r)
        pairs = beside(own, sides[r])
        first = operator(0, r, own, pairs[0], basis_row(r - 1), basis_row(r + 1))
        image[0, r + 1] = first if 0 <= r < ROWS else valid(0, r, first)
        if 0 <= r < ROWS:
            second = operator(1, r, sides[r], pairs[1], sides[r - 1], sides[r + 1])
            image[1, r + 1] = valid(1, r, second)

    for s in range(ROWS):
        at = slice(LANES * s, LANES * (s + 1))
        field = search[:, s, :]
        pairs = beside(field, side_tile(*search_sides, s))
        x_low = lo[64:96, :] if s == 0 else search[:, s - 1, :]
        x_high = hi[64:96, :] if s == ROWS - 1 else search[:, s + 1, :]
        stack[128:160, at] = operator(0, s, field, pairs[0], x_low, x_high)
        own = image[0, s + 1]
        pairs = beside(own, image[1, s + 1])
        stack[96:128, at] = operator(0, s, own, pairs[0], image[0, s], image[0, s + 2])
        stack[0:32, at] = basis[:, s, :]
        stack[32:64, at] = own
        stack[64:96, at] = field
        fields[0:32, at] = basis[:, s, :]
        fields[32:64, at] = own
        fields[64:96, at] = field

    product = dot_nt(stack[0:96, :], stack[...])
    blocks = [[product[32 * i : 32 * i + 32, 32 * j : 32 * j + 32] for j in range(5)] for i in range(3)]
    lower = lanes((32, 32)) <= lax.broadcasted_iota(jnp.int32, (32, 32), 0)
    first = jnp.where(lower, blocks[0][0], blocks[2][2])
    second = jnp.where(lower, blocks[1][1], blocks[2][4])
    sums[0:32, :] = jnp.concatenate([first, blocks[0][1], blocks[0][2], blocks[2][3]], 1)
    for k, block in enumerate((second, blocks[1][2], blocks[1][3])):
        pieces = [block[8 * q : 8 * q + 8] for q in range(4)]
        sums[32 + 8 * k : 40 + 8 * k, :] = jnp.concatenate(pieces, 1)
    rest = jnp.zeros((1, 64), jnp.float32)
    sums[56:57, :] = jnp.concatenate([diagonal(blocks[2][2]), diagonal(blocks[2][4]), rest], 1)
    sums[57:64, :] = jnp.zeros((7, LANES), jnp.float32)


def diagonal(block):
    here = lanes((32, 32)) == lax.broadcasted_iota(jnp.int32, (32, 32), 0)
    return jnp.sum(jnp.where(here, block, 0.0), 0, keepdims=True)


def parted(mixed, ends):
    turned = mixed.T
    lane = lanes((32, 32))
    row = lax.broadcasted_iota(jnp.int32, (32, 32), 0)
    upper = jnp.where(lane > row, mixed, turned)
    return jnp.where(lane <= row, mixed, turned), jnp.where(lane == row, ends, upper)


def eliminate(slabs):
    slabs = list(slabs)
    count = len(slabs)
    tile = (8, LANES)
    lane = lanes(tile)
    row = lax.broadcasted_iota(jnp.int32, tile, 0)
    width = 4
    for start in range(0, 8 * count, width):
        g, at = divmod(start, 8)
        cols = [
            [jnp.broadcast_to(slab[:, start + k : start + k + 1], tile) for slab in slabs[g:]]
            for k in range(width)
        ]
        block = [
            [jnp.broadcast_to(cols[k][0][at + m : at + m + 1, :], tile) for k in range(m + 1)]
            for m in range(width)
        ]
        rows = [jnp.broadcast_to(slabs[g][at + m : at + m + 1, :], tile) for m in range(width)]
        for k in range(width):
            here = lane == start + k
            root = lax.rsqrt(block[k][k])
            inverse = root * root
            scaled = jnp.where(here, 1.0, rows[k]) * inverse
            rows[k] = jnp.where(here, 1.0, rows[k]) * root
            column = [block[m][k] for m in range(width)[k + 1 :]]
            later = [entry * inverse for entry in column]
            for m in range(k + 1, width):
                rows[m] = jnp.where(here, 0.0, rows[m]) - column[m - k - 1] * scaled
                for n in range(k + 1, m + 1):
                    block[m][n] = block[m][n] - (column[m - k - 1] * column[n - k - 1]) * inverse
            for i in range(len(cols[k])):
                factor = cols[k][i]
                fresh = jnp.where(here, 0.0, slabs[g + i]) - factor * scaled
                slabs[g + i] = jnp.where(row >= at + width, fresh, slabs[g]) if i == 0 else fresh
                for m in range(k + 1, width):
                    cols[m][i] = cols[m][i] - factor * later[m - k - 1]
        for k in range(width):
            slabs[g] = jnp.where(row == at + k, rows[k], slabs[g])
    return slabs


def lower_part(slabs, size):
    whole = jnp.concatenate(slabs, 0)
    row = lax.broadcasted_iota(jnp.int32, whole.shape, 0)
    return jnp.where(lanes(whole.shape) <= row, whole, 0.0)[:, :size]


def update(scale, sums, start, fields, new_basis, new_search, values):
    first = sums[0:32, :] * scale
    second = sums[32:64, :] * scale
    mixed, xy, xp, pz = (first[:, 32 * k : 32 * k + 32] for k in range(4))
    other, yp, yz = (
        jnp.concatenate([second[8 * k : 8 * k + 8, 32 * q : 32 * q + 32] for q in range(4)], 0)
        for k in range(3)
    )
    xx, pp = parted(mixed, second[24:25, 0:32])
    yy, pr = parted(other, second[24:25, 32:64])
    px, py, zp = xp.T, yp.T, pz.T
    zero = jnp.zeros((32, 32), jnp.float32)
    gram = [
        jnp.concatenate([xx, xy, xp, zero], 1),
        jnp.concatenate([xy, yy, yp, zero], 1),
        jnp.concatenate([px, py, pp, zero], 1),
    ]
    projected = jnp.concatenate(
        [
            jnp.concatenate([xy, yy, yp], 1),
            jnp.concatenate([yy, yz, zp], 1),
            jnp.concatenate([py, pz, pr], 1),
        ],
        0,
    )
    lower_inv = lower_part(
        eliminate([block[8 * k : 8 * k + 8] for block in gram for k in range(4)]), 96
    )
    half = dot_nn(lower_inv, projected)
    ritz = 0.5 * (dot_nt(half, lower_inv) + dot_nt(lower_inv, half))
    bound = jnp.max(jnp.sum(jnp.abs(ritz), 0, keepdims=True), 1, keepdims=True)
    seed = start[...].astype(jnp.float32)
    moved = bound * seed - dot_nn(seed, ritz)
    square = jnp.concatenate([dot_nt(moved, moved), jnp.zeros((32, 96), jnp.float32)], 1)
    weights = dot_nn(moved, lower_inv)
    quotient = diagonal(xy) / diagonal(xx)
    middle = weights[:, 32:64]
    search_weights = jnp.concatenate([-(middle * quotient), middle, weights[:, 64:96]], 1)
    mixed_fields = dot_nn(jnp.concatenate([weights, search_weights], 0), fields[...])
    mixed_ritz = dot_nn(moved, ritz)
    small_inv = lower_part(eliminate([square[8 * k : 8 * k + 8] for k in range(4)]), 32)
    both = jnp.concatenate([mixed_fields[0:32], mixed_fields[32:64]], 1)
    result = dot_nn(small_inv, both)
    terms = dot_nn(small_inv, moved) * dot_nn(small_inv, mixed_ritz)
    values[...] = dot_nt(jnp.ones((8, 96), jnp.float32), terms)[0:1, :]
    wide = ROWS * LANES
    for s in range(ROWS):
        new_basis[:, s, :] = result[:, LANES * s : LANES * (s + 1)]
        new_search[:, s, :] = result[:, wide + LANES * s : wide + LANES * (s + 1)]


def call(kernel, outs, *args, scratch=(), place=VMEM):
    shapes = [jax.ShapeDtypeStruct(shape, jnp.float32) for shape in outs]
    return pl.pallas_call(
        kernel,
        out_shape=shapes,
        in_specs=[place] * len(args),
        out_specs=[VMEM] * len(shapes),
        scratch_shapes=[
            pltpu.VMEM(shape, jnp.float32) if isinstance(shape, tuple) else shape for shape in scratch
        ],
        compiler_params=pltpu.CompilerParams(vmem_limit_bytes=32 * 1024 * 1024),
    )(*args)


def paired(array, axis, first):
    pairs = [(i, i + 1) for i in range(first, lax.axis_size(axis) - 1, 2)]
    return lax.ppermute(array, axis, pairs + [(j, i) for i, j in pairs])


def exchanged(array, axis):
    return lax.all_to_all(array, axis, 0, 0, tiled=True)


def summed(array, count):
    return jnp.sum(array.reshape(count, array.shape[0] // count, LANES), 0)


def total(array):
    across, along = lax.axis_size("gy"), lax.axis_size("gx")
    share = summed(exchanged(array, "gy"), across)
    share = summed(exchanged(jnp.tile(share, (along, 1)), "gx"), along)
    return exchanged(jnp.tile(share, (across, 1)), "gy")


def body(basis, search, conductivity, rotation):
    modes, cells_x, flat = basis.shape
    count = cells_x * flat * lax.axis_size("gx") * lax.axis_size("gy")
    blocks = [basis.shape, search.shape, conductivity.shape]
    rows = call(
        pack_rows,
        [(104, LANES)] * 2,
        *(pltpu.with_memory_space_constraint(x, pltpu.HBM) for x in (basis, search, conductivity)),
        scratch=blocks + [pltpu.SemaphoreType.DMA((3,))],
        place=pl.BlockSpec(memory_space=pltpu.HBM),
    )
    row_two = paired(rows[1], "gx", 1)
    row_one = paired(rows[0], "gx", 0)
    side_one, side_two, lo, hi = call(
        pack_sides,
        [(112, LANES)] * 2 + [(104, LANES)] * 2,
        basis,
        search,
        conductivity,
        row_two,
        row_one,
        scratch=[(112, LANES)] * 2,
    )
    side_two = paired(side_two, "gy", 1)
    side_one = paired(side_one, "gy", 0)
    fields, sums = call(
        images,
        [(96, ROWS * LANES), (64, LANES)],
        basis,
        search,
        conductivity,
        lo,
        hi,
        side_two,
        side_one,
        scratch=[(2, 24, LANES), (2, 5, 16, LANES), (2, 10, MODES, LANES), (160, ROWS * LANES)]
        + [(112, LANES)] * 2,
    )
    sums = total(sums)

    def finish(*refs):
        update(1.0 / count, *refs)

    new_basis, new_search, values = call(
        finish,
        [(modes, cells_x, flat), (modes, cells_x, flat), (1, modes)],
        sums,
        rotation.T,
        fields,
    )
    return new_basis, new_search, values.reshape(modes)


def solution(mesh):
    in_specs = (P(None, "gx", "gy"), P(None, "gx", "gy"), P("gx", "gy"), P())
    out_specs = (P(None, "gx", "gy"), P(None, "gx", "gy"), P())
    return jax.shard_map(body, mesh=mesh, in_specs=in_specs, out_specs=out_specs, check_vma=False)
```

```python
import jax
import jax.numpy as jnp
from jax import lax
from jax.experimental import pallas as pl
from jax.experimental.pallas import tpu as pltpu
from jax.sharding import PartitionSpec as P

CZ = 16
MODES = 32
ROWS = 8
LANES = 128
HIGH = lax.Precision.HIGHEST
VMEM = pl.BlockSpec(memory_space=pltpu.VMEM)


def dot_nt(left, right):
    return lax.dot_general(
        left, right, (((1,), (1,)), ((), ())), precision=HIGH, preferred_element_type=jnp.float32
    )


def dot_nn(left, right):
    return lax.dot_general(
        left, right, (((1,), (0,)), ((), ())), precision=HIGH, preferred_element_type=jnp.float32
    )


def roll(array, shift):
    shift = shift % LANES
    return pltpu.roll(array, shift, array.ndim - 1) if shift else array


def lanes(shape):
    return lax.broadcasted_iota(jnp.int32, shape, len(shape) - 1)


def is_odd(axis):
    return lax.axis_index(axis) % 2 == 1


def sort_sides(axis, one, two, low, high):
    odd = is_odd(axis)
    low[...] = jnp.where(odd, one[...], two[...])
    high[...] = jnp.where(odd, two[...], one[...])


def pack_rows(basis_hbm, search_hbm, cond_hbm, one, two, basis, search, cond, arrived):
    copies = [
        pltpu.make_async_copy(source, target, arrived.at[k])
        for k, (source, target) in enumerate(
            ((basis_hbm, basis), (search_hbm, search), (cond_hbm, cond))
        )
    ]
    for copy in copies:
        copy.start()
    for copy in copies:
        copy.wait()
    up = [basis[:, 6, :], basis[:, 7, :], search[:, 7, :]]
    down = [basis[:, 0, :], basis[:, 1, :], search[:, 0, :]]
    odd = is_odd("gx")
    for k in range(3):
        one[32 * k : 32 * k + 32, :] = jnp.where(odd, down[k], up[k])
        two[32 * k : 32 * k + 32, :] = jnp.where(odd, up[k], down[k])
    one[96:104, :] = cond[...]
    two[96:104, :] = cond[...]


def pack_layers(rows, right):
    lane = lanes(rows[0].shape) // CZ
    outer = second = None
    for s in range(ROWS):
        moved = roll(rows[s], CZ * (s + 1 if right else s))
        at = (s - 1 if right else s + 1) % ROWS
        outer = moved if outer is None else jnp.where(lane == s, moved, outer)
        second = moved if second is None else jnp.where(lane == at, moved, second)
    return outer, second


def pack_ends(before, after, right):
    before = roll(before, CZ if right else 0)
    after = roll(after, 2 * CZ if right else CZ)
    return jnp.where(lanes(before.shape) < CZ, before, after)


def pack_sides(basis, search, cond, row_two, row_one, side_one, side_two, lo, hi, right, left):
    sort_sides("gx", row_one, row_two, lo, hi)
    block = (8, LANES)
    field = [basis[:, s, :] for s in range(ROWS)]
    other = [search[:, s, :] for s in range(ROWS)]
    cells = [jnp.broadcast_to(cond[s : s + 1, :], block) for s in range(ROWS)]
    cell_lo = jnp.broadcast_to(lo[103:104, :], block)
    cell_hi = jnp.broadcast_to(hi[96:97, :], block)
    lane = lanes(block)
    for message, to_right in ((right, True), (left, False)):
        message[0:32, :], message[32:64, :] = pack_layers(field, to_right)
        message[64:96, :] = pack_layers(other, to_right)[0]
        ends = pack_ends(lo[32:64, :], hi[0:32, :], to_right)
        folded = ends[0:8]
        for q in range(1, 4):
            folded = jnp.where(lane >= 32 * q, roll(ends[8 * q : 8 * q + 8], 32 * q), folded)
        message[96:104, :] = folded
        cell_outer, cell_second = pack_layers(cells, to_right)
        message[104:105, :] = cell_outer[:1]
        message[105:106, :] = cell_second[:1]
        message[106:107, :] = pack_ends(cell_lo, cell_hi, to_right)[:1]
        message[107:112, :] = jnp.zeros((5, LANES), jnp.float32)
    sort_sides("gy", left, right, side_one, side_two)


def side_tile(low, high, s):
    lane = lanes(low[0].shape) // CZ
    if 0 <= s < ROWS:
        above = [roll(part, -CZ * s) for part in high[:2]]
        below = [roll(part, CZ * (7 - s)) for part in low[:2]]
        tile = jnp.where(lane == 0, above[0], jnp.where(lane == 7, below[0], 0.0))
        if len(above) == 2:
            tile = jnp.where(lane == 1, above[1], jnp.where(lane == 6, below[1], tile))
        return tile
    k = 0 if s < 0 else 1
    above, below = roll(high[2], -CZ * k), roll(low[2], CZ * (7 - k))
    return jnp.where(lane == 0, above, jnp.where(lane == 7, below, 0.0))


def unfolded(folded):
    return jnp.concatenate([roll(folded, -32 * q) for q in range(4)], 0)


def next_y(own, side):
    lane = lanes(own.shape)
    a, b = roll(own, -CZ), roll(side, -CZ)
    return jnp.where(lane < LANES - CZ, a, b), jnp.where(lane < LANES - CZ, b, a)


def prev_y(own, side):
    lane = lanes(own.shape)
    a, b = roll(own, CZ), roll(side, CZ)
    return jnp.where(lane >= CZ, a, b), jnp.where(lane >= CZ, b, a)


def next_z(array):
    return jnp.where(lanes(array.shape) % CZ == CZ - 1, roll(array, CZ - 1), roll(array, -1))


def prev_z(array):
    return jnp.where(lanes(array.shape) % CZ == 0, roll(array, 1 - CZ), roll(array, 1))


def inner(basis, search, cond, image, other, coef):
    lane = lanes((ROWS, LANES))
    cells = cond[...]
    after, before = roll(cells, -CZ), roll(cells, CZ)
    coef[0] = jnp.where(lane < LANES - CZ, 0.5 * (cells + after), 0.0)
    coef[1] = jnp.where(lane >= CZ, 0.5 * (cells + before), 0.0)
    coef[2] = 0.5 * (cells + next_z(cells))
    coef[3] = 0.5 * (cells + prev_z(cells))
    for field, result in ((basis, image), (search, other)):
        flux = None
        for s in range(ROWS):
            own = field[:, s, :]
            total = coef[0, s : s + 1, :] * (own - roll(own, -CZ))
            total += coef[1, s : s + 1, :] * (own - roll(own, CZ))
            total += coef[2, s : s + 1, :] * (own - next_z(own))
            total += coef[3, s : s + 1, :] * (own - prev_z(own))
            if s > 0:
                total += flux
            if s < ROWS - 1:
                face = 0.5 * (cond[s : s + 1, :] + cond[s + 1 : s + 2, :])
                flux = face * (field[:, s + 1, :] - own)
                total -= flux
            result[s] = total


def images(
    basis, search, cond, inner_x, inner_p, lo, hi, side_two, side_one, fields, sums, conds, coef, image, stack, low, high
):
    sort_sides("gy", side_one, side_two, low, high)
    basis_sides = [(part[0:32, :], part[32:64, :], unfolded(part[96:104, :])) for part in (low, high)]
    search_sides = [(part[64:96, :],) for part in (low, high)]
    cond_sides = [
        [jnp.broadcast_to(part[r : r + 1, :], (8, LANES)) for r in range(104, 107)] for part in (low, high)
    ]
    conds[...] = jnp.zeros_like(conds)
    conds[0, 0:2, :] = lo[102:104, :]
    conds[0, 2:10, :] = cond[...]
    conds[0, 10:12, :] = hi[96:98, :]
    for r in range(10):
        conds[1, r + 1 : r + 2, :] = side_tile(*cond_sides, r - 1)[:1]
    cond_a, cond_b = conds[0, 0:16, :], conds[1, 0:16, :]
    after = next_y(cond_a, cond_b)
    before = prev_y(cond_a, cond_b)
    for part, array in ((0, cond_a), (1, cond_b)):
        coef[part, 0] = 0.5 * (array + conds[part, 1:17, :])
        coef[part, 1] = 0.5 * (array + after[part])
        coef[part, 2] = 0.5 * (array + before[part])
        coef[part, 3] = 0.5 * (array + next_z(array))
        coef[part, 4] = 0.5 * (array + prev_z(array))

    def operator(part, r, own, beside, x_low, x_high):
        i = r + 2
        total = coef[part, 0, i - 1 : i, :] * (own - x_low)
        total += coef[part, 0, i : i + 1, :] * (own - x_high)
        total += coef[part, 1, i : i + 1, :] * (own - beside[0])
        total += coef[part, 2, i : i + 1, :] * (own - beside[1])
        total += coef[part, 3, i : i + 1, :] * (own - next_z(own))
        total += coef[part, 4, i : i + 1, :] * (own - prev_z(own))
        return total

    def outer(s, own, side, x_low, x_high):
        i = s + 2
        group = lanes(own.shape) // CZ
        other = jnp.where(group == 0, roll(side, CZ), roll(side, -CZ))
        first = lanes((1, LANES)) // CZ
        face = jnp.where(first == 0, coef[0, 2, i : i + 1, :], 0.0)
        face = jnp.where(first == 7, coef[0, 1, i : i + 1, :], face)
        total = face * (own - other)
        if s == 0:
            total += coef[0, 0, i - 1 : i, :] * (own - x_low)
        if s == ROWS - 1:
            total += coef[0, 0, i : i + 1, :] * (own - x_high)
        return total

    def beside(own, side):
        after, before = next_y(own, side), prev_y(own, side)
        return ((after[0], before[0]), (after[1], before[1]))

    def basis_row(r):
        if r < 0:
            return lo[32 * (r + 2) : 32 * (r + 3), :]
        if r >= ROWS:
            return hi[32 * (r - ROWS) : 32 * (r - ROWS + 1), :]
        return basis[:, r, :]

    def valid(part, r, array):
        return jnp.where(conds[part, r + 2 : r + 3, :] > 0.0, array, 0.0)

    sides = {r: side_tile(*basis_sides, r) for r in range(-1, 2)}
    for r in range(-1, ROWS + 1):
        if 1 <= r < ROWS:
            sides[r + 1] = side_tile(*basis_sides, r + 1)
        own = basis_row(r)
        pairs = beside(own, sides[r])
        if 0 <= r < ROWS:
            image[0, r + 1] = inner_x[r] + outer(r, own, sides[r], basis_row(-1), basis_row(ROWS))
        else:
            first = operator(0, r, own, pairs[0], basis_row(r - 1), basis_row(r + 1))
            image[0, r + 1] = valid(0, r, first)
        if 0 <= r < ROWS:
            second = operator(1, r, sides[r], pairs[1], sides[r - 1], sides[r + 1])
            image[1, r + 1] = valid(1, r, second)

    for s in range(ROWS):
        at = slice(LANES * s, LANES * (s + 1))
        field = search[:, s, :]
        side = side_tile(*search_sides, s)
        stack[128:160, at] = inner_p[s] + outer(s, field, side, lo[64:96, :], hi[64:96, :])
        own = image[0, s + 1]
        pairs = beside(own, image[1, s + 1])
        stack[96:128, at] = operator(0, s, own, pairs[0], image[0, s], image[0, s + 2])
        stack[0:32, at] = basis[:, s, :]
        stack[32:64, at] = own
        stack[64:96, at] = field
        fields[0:32, at] = basis[:, s, :]
        fields[32:64, at] = own
        fields[64:96, at] = field

    product = dot_nt(stack[0:96, :], stack[...])
    blocks = [[product[32 * i : 32 * i + 32, 32 * j : 32 * j + 32] for j in range(5)] for i in range(3)]
    lower = lanes((32, 32)) <= lax.broadcasted_iota(jnp.int32, (32, 32), 0)
    first = jnp.where(lower, blocks[0][0], blocks[2][2])
    second = jnp.where(lower, blocks[1][1], blocks[2][4])
    sums[0:32, :] = jnp.concatenate([first, blocks[0][1], blocks[0][2], blocks[2][3]], 1)
    for k, block in enumerate((second, blocks[1][2], blocks[1][3])):
        pieces = [block[8 * q : 8 * q + 8] for q in range(4)]
        sums[32 + 8 * k : 40 + 8 * k, :] = jnp.concatenate(pieces, 1)
    rest = jnp.zeros((1, 64), jnp.float32)
    sums[56:57, :] = jnp.concatenate([diagonal(blocks[2][2]), diagonal(blocks[2][4]), rest], 1)
    sums[57:64, :] = jnp.zeros((7, LANES), jnp.float32)


def diagonal(block):
    here = lanes((32, 32)) == lax.broadcasted_iota(jnp.int32, (32, 32), 0)
    return jnp.sum(jnp.where(here, block, 0.0), 0, keepdims=True)


def parted(mixed, ends):
    turned = mixed.T
    lane = lanes((32, 32))
    row = lax.broadcasted_iota(jnp.int32, (32, 32), 0)
    upper = jnp.where(lane > row, mixed, turned)
    return jnp.where(lane <= row, mixed, turned), jnp.where(lane == row, ends, upper)


def eliminate(slabs):
    slabs = list(slabs)
    count = len(slabs)
    lane = lanes((8, LANES))
    row = lax.broadcasted_iota(jnp.int32, (8, LANES), 0)
    width = 4
    for start in range(0, 8 * count, width):
        g = start // 8
        cols = [
            {i: jnp.broadcast_to(slabs[i][:, start + k : start + k + 1], (8, LANES)) for i in range(g, count)}
            for k in range(width)
        ]
        for k in range(width):
            j = start + k
            at = j % 8
            pivot = cols[k][g][at : at + 1, :]
            root = lax.rsqrt(pivot)
            inverse = root * root
            here = lane[:1] == j
            pivot_row = jnp.where(here, 1.0, slabs[g][at : at + 1, :])
            scaled = pivot_row * inverse
            later = [cols[m][g][at : at + 1, :] * inverse for m in range(k + 1, width)]
            for i in range(g, count):
                factor = cols[k][i]
                kept = jnp.where(lane == j, 0.0, slabs[i])
                if i == g:
                    factor = jnp.where(row > at, factor, 0.0)
                    kept = jnp.where(row > at, kept, slabs[i])
                    fresh = kept - factor * scaled
                    slabs[i] = jnp.where(row == at, pivot_row * root, fresh)
                else:
                    slabs[i] = kept - factor * scaled
                for m in range(k + 1, width):
                    cols[m][i] = cols[m][i] - factor * later[m - k - 1]
    return slabs


def lower_part(slabs, size):
    whole = jnp.concatenate(slabs, 0)
    row = lax.broadcasted_iota(jnp.int32, whole.shape, 0)
    return jnp.where(lanes(whole.shape) <= row, whole, 0.0)[:, :size]


def update(scale, sums, start, fields, new_basis, new_search, values):
    first = sums[0:32, :] * scale
    second = sums[32:64, :] * scale
    mixed, xy, xp, pz = (first[:, 32 * k : 32 * k + 32] for k in range(4))
    other, yp, yz = (
        jnp.concatenate([second[8 * k : 8 * k + 8, 32 * q : 32 * q + 32] for q in range(4)], 0)
        for k in range(3)
    )
    xx, pp = parted(mixed, second[24:25, 0:32])
    yy, pr = parted(other, second[24:25, 32:64])
    px, py, zp = xp.T, yp.T, pz.T
    zero = jnp.zeros((32, 32), jnp.float32)
    gram = [
        jnp.concatenate([xx, xy, xp, zero], 1),
        jnp.concatenate([xy, yy, yp, zero], 1),
        jnp.concatenate([px, py, pp, zero], 1),
    ]
    projected = jnp.concatenate(
        [
            jnp.concatenate([xy, yy, yp], 1),
            jnp.concatenate([yy, yz, zp], 1),
            jnp.concatenate([py, pz, pr], 1),
        ],
        0,
    )
    lower_inv = lower_part(
        eliminate([block[8 * k : 8 * k + 8] for block in gram for k in range(4)]), 96
    )
    half = dot_nn(lower_inv, projected)
    ritz = 0.5 * (dot_nt(half, lower_inv) + dot_nt(lower_inv, half))
    bound = jnp.max(jnp.sum(jnp.abs(ritz), 0, keepdims=True), 1, keepdims=True)
    seed = start[...].astype(jnp.float32)
    moved = bound * seed - dot_nn(seed, ritz)
    square = jnp.concatenate([dot_nt(moved, moved), jnp.zeros((32, 96), jnp.float32)], 1)
    weights = dot_nn(moved, lower_inv)
    quotient = diagonal(xy) / diagonal(xx)
    middle = weights[:, 32:64]
    search_weights = jnp.concatenate([-(middle * quotient), middle, weights[:, 64:96]], 1)
    mixed_fields = dot_nn(jnp.concatenate([weights, search_weights], 0), fields[...])
    mixed_ritz = dot_nn(moved, ritz)
    small_inv = lower_part(eliminate([square[8 * k : 8 * k + 8] for k in range(4)]), 32)
    both = jnp.concatenate([mixed_fields[0:32], mixed_fields[32:64]], 1)
    result = dot_nn(small_inv, both)
    terms = dot_nn(small_inv, moved) * dot_nn(small_inv, mixed_ritz)
    values[...] = dot_nt(jnp.ones((8, 96), jnp.float32), terms)[0:1, :]
    wide = ROWS * LANES
    for s in range(ROWS):
        new_basis[:, s, :] = result[:, LANES * s : LANES * (s + 1)]
        new_search[:, s, :] = result[:, wide + LANES * s : wide + LANES * (s + 1)]


def call(kernel, outs, *args, scratch=(), place=VMEM, cost=None):
    shapes = [jax.ShapeDtypeStruct(shape, jnp.float32) for shape in outs]
    return pl.pallas_call(
        kernel,
        out_shape=shapes,
        in_specs=[place] * len(args),
        cost_estimate=cost,
        out_specs=[VMEM] * len(shapes),
        scratch_shapes=[
            pltpu.VMEM(shape, jnp.float32) if isinstance(shape, tuple) else shape for shape in scratch
        ],
        compiler_params=pltpu.CompilerParams(vmem_limit_bytes=32 * 1024 * 1024),
    )(*args)


def paired(array, axis, first):
    pairs = [(i, i + 1) for i in range(first, lax.axis_size(axis) - 1, 2)]
    return lax.ppermute(array, axis, pairs + [(j, i) for i, j in pairs])


def exchanged(array, axis):
    return lax.all_to_all(array, axis, 0, 0, tiled=True)


def summed(array, count):
    return jnp.sum(array.reshape(count, array.shape[0] // count, LANES), 0)


def total(array):
    across, along = lax.axis_size("gy"), lax.axis_size("gx")
    share = summed(exchanged(array, "gy"), across)
    share = summed(exchanged(jnp.tile(share, (along, 1)), "gx"), along)
    return exchanged(jnp.tile(share, (across, 1)), "gy")


def body(basis, search, conductivity, rotation):
    modes, cells_x, flat = basis.shape
    count = cells_x * flat * lax.axis_size("gx") * lax.axis_size("gy")
    blocks = [basis.shape, search.shape, conductivity.shape]
    rows = call(
        pack_rows,
        [(104, LANES)] * 2,
        *(pltpu.with_memory_space_constraint(x, pltpu.HBM) for x in (basis, search, conductivity)),
        scratch=blocks + [pltpu.SemaphoreType.DMA((3,))],
        place=pl.BlockSpec(memory_space=pltpu.HBM),
    )
    inner_x, inner_p = call(
        inner,
        [(cells_x, modes, flat)] * 2,
        basis,
        search,
        conductivity,
        scratch=[(4, ROWS, LANES)],
        cost=pl.CostEstimate(flops=4 << 20, bytes_accessed=1 << 20, transcendentals=0),
    )
    row_two = paired(rows[1], "gx", 1)
    row_one = paired(rows[0], "gx", 0)
    side_one, side_two, lo, hi = call(
        pack_sides,
        [(112, LANES)] * 2 + [(104, LANES)] * 2,
        basis,
        search,
        conductivity,
        row_two,
        row_one,
        scratch=[(112, LANES)] * 2,
    )
    side_two = paired(side_two, "gy", 1)
    side_one = paired(side_one, "gy", 0)
    fields, sums = call(
        images,
        [(96, ROWS * LANES), (64, LANES)],
        basis,
        search,
        conductivity,
        inner_x,
        inner_p,
        lo,
        hi,
        side_two,
        side_one,
        scratch=[(2, 24, LANES), (2, 5, 16, LANES), (2, 10, MODES, LANES), (160, ROWS * LANES)]
        + [(112, LANES)] * 2,
    )
    sums = total(sums)

    def finish(*refs):
        update(1.0 / count, *refs)

    new_basis, new_search, values = call(
        finish,
        [(modes, cells_x, flat), (modes, cells_x, flat), (1, modes)],
        sums,
        rotation.T,
        fields,
    )
    return new_basis, new_search, values.reshape(modes)


def solution(mesh):
    in_specs = (P(None, "gx", "gy"), P(None, "gx", "gy"), P("gx", "gy"), P())
    out_specs = (P(None, "gx", "gy"), P(None, "gx", "gy"), P())
    return jax.shard_map(body, mesh=mesh, in_specs=in_specs, out_specs=out_specs, check_vma=False)
```

```python
import jax
import jax.numpy as jnp
from jax import lax
from jax.experimental import pallas as pl
from jax.experimental.pallas import tpu as pltpu
from jax.sharding import PartitionSpec as P

CZ = 16
MODES = 32
ROWS = 8
LANES = 128
HIGH = lax.Precision.HIGHEST
VMEM = pl.BlockSpec(memory_space=pltpu.VMEM)


def dot_nt(left, right):
    return lax.dot_general(
        left, right, (((1,), (1,)), ((), ())), precision=HIGH, preferred_element_type=jnp.float32
    )


def dot_nn(left, right):
    return lax.dot_general(
        left, right, (((1,), (0,)), ((), ())), precision=HIGH, preferred_element_type=jnp.float32
    )


def roll(array, shift):
    shift = shift % LANES
    return pltpu.roll(array, shift, array.ndim - 1) if shift else array


def lanes(shape):
    return lax.broadcasted_iota(jnp.int32, shape, len(shape) - 1)


def is_odd(axis):
    return lax.axis_index(axis) % 2 == 1


def sort_sides(axis, one, two, low, high):
    odd = is_odd(axis)
    low[...] = jnp.where(odd, one[...], two[...])
    high[...] = jnp.where(odd, two[...], one[...])


def pack_rows(basis_hbm, search_hbm, cond_hbm, one, two, basis, search, cond, arrived):
    copies = [
        pltpu.make_async_copy(source, target, arrived.at[k])
        for k, (source, target) in enumerate(
            ((basis_hbm, basis), (search_hbm, search), (cond_hbm, cond))
        )
    ]
    for copy in copies:
        copy.start()
    for copy in copies:
        copy.wait()
    up = [basis[:, 6, :], basis[:, 7, :], search[:, 7, :]]
    down = [basis[:, 0, :], basis[:, 1, :], search[:, 0, :]]
    odd = is_odd("gx")
    for k in range(3):
        one[32 * k : 32 * k + 32, :] = jnp.where(odd, down[k], up[k])
        two[32 * k : 32 * k + 32, :] = jnp.where(odd, up[k], down[k])
    one[96:104, :] = cond[...]
    two[96:104, :] = cond[...]


def pack_layers(rows, right):
    lane = lanes(rows[0].shape) // CZ
    outer = second = None
    for s in range(ROWS):
        moved = roll(rows[s], CZ * (s + 1 if right else s))
        at = (s - 1 if right else s + 1) % ROWS
        outer = moved if outer is None else jnp.where(lane == s, moved, outer)
        second = moved if second is None else jnp.where(lane == at, moved, second)
    return outer, second


def pack_ends(before, after, right):
    before = roll(before, CZ if right else 0)
    after = roll(after, 2 * CZ if right else CZ)
    return jnp.where(lanes(before.shape) < CZ, before, after)


def pack_sides(basis, search, cond, row_two, row_one, side_one, side_two, lo, hi, right, left):
    sort_sides("gx", row_one, row_two, lo, hi)
    block = (8, LANES)
    field = [basis[:, s, :] for s in range(ROWS)]
    other = [search[:, s, :] for s in range(ROWS)]
    cells = [jnp.broadcast_to(cond[s : s + 1, :], block) for s in range(ROWS)]
    cell_lo = jnp.broadcast_to(lo[103:104, :], block)
    cell_hi = jnp.broadcast_to(hi[96:97, :], block)
    lane = lanes(block)
    for message, to_right in ((right, True), (left, False)):
        message[0:32, :], message[32:64, :] = pack_layers(field, to_right)
        message[64:96, :] = pack_layers(other, to_right)[0]
        ends = pack_ends(lo[32:64, :], hi[0:32, :], to_right)
        folded = ends[0:8]
        for q in range(1, 4):
            folded = jnp.where(lane >= 32 * q, roll(ends[8 * q : 8 * q + 8], 32 * q), folded)
        message[96:104, :] = folded
        cell_outer, cell_second = pack_layers(cells, to_right)
        message[104:105, :] = cell_outer[:1]
        message[105:106, :] = cell_second[:1]
        message[106:107, :] = pack_ends(cell_lo, cell_hi, to_right)[:1]
        message[107:112, :] = jnp.zeros((5, LANES), jnp.float32)
    sort_sides("gy", left, right, side_one, side_two)


def side_tile(low, high, s):
    lane = lanes(low[0].shape) // CZ
    if 0 <= s < ROWS:
        above = [roll(part, -CZ * s) for part in high[:2]]
        below = [roll(part, CZ * (7 - s)) for part in low[:2]]
        tile = jnp.where(lane == 0, above[0], jnp.where(lane == 7, below[0], 0.0))
        if len(above) == 2:
            tile = jnp.where(lane == 1, above[1], jnp.where(lane == 6, below[1], tile))
        return tile
    k = 0 if s < 0 else 1
    above, below = roll(high[2], -CZ * k), roll(low[2], CZ * (7 - k))
    return jnp.where(lane == 0, above, jnp.where(lane == 7, below, 0.0))


def unfolded(folded):
    return jnp.concatenate([roll(folded, -32 * q) for q in range(4)], 0)


def next_y(own, side):
    lane = lanes(own.shape)
    a, b = roll(own, -CZ), roll(side, -CZ)
    return jnp.where(lane < LANES - CZ, a, b), jnp.where(lane < LANES - CZ, b, a)


def prev_y(own, side):
    lane = lanes(own.shape)
    a, b = roll(own, CZ), roll(side, CZ)
    return jnp.where(lane >= CZ, a, b), jnp.where(lane >= CZ, b, a)


def next_z(array):
    return jnp.where(lanes(array.shape) % CZ == CZ - 1, roll(array, CZ - 1), roll(array, -1))


def prev_z(array):
    return jnp.where(lanes(array.shape) % CZ == 0, roll(array, 1 - CZ), roll(array, 1))


def inner(basis, search, cond, image, other, coef):
    lane = lanes((ROWS, LANES))
    cells = cond[...]
    after, before = roll(cells, -CZ), roll(cells, CZ)
    coef[0] = jnp.where(lane < LANES - CZ, 0.5 * (cells + after), 0.0)
    coef[1] = jnp.where(lane >= CZ, 0.5 * (cells + before), 0.0)
    coef[2] = 0.5 * (cells + next_z(cells))
    coef[3] = 0.5 * (cells + prev_z(cells))
    for field, result in ((basis, image), (search, other)):
        flux = None
        for s in range(ROWS):
            own = field[:, s, :]
            total = coef[0, s : s + 1, :] * (own - roll(own, -CZ))
            total += coef[1, s : s + 1, :] * (own - roll(own, CZ))
            total += coef[2, s : s + 1, :] * (own - next_z(own))
            total += coef[3, s : s + 1, :] * (own - prev_z(own))
            if s > 0:
                total += flux
            if s < ROWS - 1:
                face = 0.5 * (cond[s : s + 1, :] + cond[s + 1 : s + 2, :])
                flux = face * (field[:, s + 1, :] - own)
                total -= flux
            result[s] = total


def images(
    basis, search, cond, inner_x, inner_p, lo, hi, side_two, side_one, fields, sums, conds, coef, image, stack, low, high
):
    sort_sides("gy", side_one, side_two, low, high)
    basis_sides = [(part[0:32, :], part[32:64, :], unfolded(part[96:104, :])) for part in (low, high)]
    search_sides = [(part[64:96, :],) for part in (low, high)]
    cond_sides = [
        [jnp.broadcast_to(part[r : r + 1, :], (8, LANES)) for r in range(104, 107)] for part in (low, high)
    ]
    conds[...] = jnp.zeros_like(conds)
    conds[0, 0:2, :] = lo[102:104, :]
    conds[0, 2:10, :] = cond[...]
    conds[0, 10:12, :] = hi[96:98, :]
    for r in range(10):
        conds[1, r + 1 : r + 2, :] = side_tile(*cond_sides, r - 1)[:1]
    cond_a, cond_b = conds[0, 0:16, :], conds[1, 0:16, :]
    after = next_y(cond_a, cond_b)
    before = prev_y(cond_a, cond_b)
    for part, array in ((0, cond_a), (1, cond_b)):
        coef[part, 0] = 0.5 * (array + conds[part, 1:17, :])
        coef[part, 1] = 0.5 * (array + after[part])
        coef[part, 2] = 0.5 * (array + before[part])
        coef[part, 3] = 0.5 * (array + next_z(array))
        coef[part, 4] = 0.5 * (array + prev_z(array))

    def operator(part, r, own, beside, x_low, x_high):
        i = r + 2
        total = coef[part, 0, i - 1 : i, :] * (own - x_low)
        total += coef[part, 0, i : i + 1, :] * (own - x_high)
        total += coef[part, 1, i : i + 1, :] * (own - beside[0])
        total += coef[part, 2, i : i + 1, :] * (own - beside[1])
        total += coef[part, 3, i : i + 1, :] * (own - next_z(own))
        total += coef[part, 4, i : i + 1, :] * (own - prev_z(own))
        return total

    def outer(s, own, side, x_low, x_high):
        i = s + 2
        group = lanes(own.shape) // CZ
        other = jnp.where(group == 0, roll(side, CZ), roll(side, -CZ))
        first = lanes((1, LANES)) // CZ
        face = jnp.where(first == 0, coef[0, 2, i : i + 1, :], 0.0)
        face = jnp.where(first == 7, coef[0, 1, i : i + 1, :], face)
        total = face * (own - other)
        if s == 0:
            total += coef[0, 0, i - 1 : i, :] * (own - x_low)
        if s == ROWS - 1:
            total += coef[0, 0, i : i + 1, :] * (own - x_high)
        return total

    def beside(own, side):
        after, before = next_y(own, side), prev_y(own, side)
        return ((after[0], before[0]), (after[1], before[1]))

    def basis_row(r):
        if r < 0:
            return lo[32 * (r + 2) : 32 * (r + 3), :]
        if r >= ROWS:
            return hi[32 * (r - ROWS) : 32 * (r - ROWS + 1), :]
        return basis[:, r, :]

    def valid(part, r, array):
        return jnp.where(conds[part, r + 2 : r + 3, :] > 0.0, array, 0.0)

    sides = {r: side_tile(*basis_sides, r) for r in range(-1, 2)}
    for r in range(-1, ROWS + 1):
        if 1 <= r < ROWS:
            sides[r + 1] = side_tile(*basis_sides, r + 1)
        own = basis_row(r)
        pairs = beside(own, sides[r])
        if 0 <= r < ROWS:
            image[0, r + 1] = inner_x[r] + outer(r, own, sides[r], basis_row(-1), basis_row(ROWS))
        else:
            first = operator(0, r, own, pairs[0], basis_row(r - 1), basis_row(r + 1))
            image[0, r + 1] = valid(0, r, first)
        if 0 <= r < ROWS:
            second = operator(1, r, sides[r], pairs[1], sides[r - 1], sides[r + 1])
            image[1, r + 1] = valid(1, r, second)

    for s in range(ROWS):
        at = slice(LANES * s, LANES * (s + 1))
        field = search[:, s, :]
        side = side_tile(*search_sides, s)
        stack[128:160, at] = inner_p[s] + outer(s, field, side, lo[64:96, :], hi[64:96, :])
        own = image[0, s + 1]
        pairs = beside(own, image[1, s + 1])
        stack[96:128, at] = operator(0, s, own, pairs[0], image[0, s], image[0, s + 2])
        stack[0:32, at] = basis[:, s, :]
        stack[32:64, at] = own
        stack[64:96, at] = field
        fields[0:32, at] = basis[:, s, :]
        fields[32:64, at] = own
        fields[64:96, at] = field

    product = dot_nt(stack[0:96, :], stack[...])
    blocks = [[product[32 * i : 32 * i + 32, 32 * j : 32 * j + 32] for j in range(5)] for i in range(3)]
    lower = lanes((32, 32)) <= lax.broadcasted_iota(jnp.int32, (32, 32), 0)
    first = jnp.where(lower, blocks[0][0], blocks[2][2])
    second = jnp.where(lower, blocks[1][1], blocks[2][4])
    sums[0:32, :] = jnp.concatenate([first, blocks[0][1], blocks[0][2], blocks[2][3]], 1)
    for k, block in enumerate((second, blocks[1][2], blocks[1][3])):
        pieces = [block[8 * q : 8 * q + 8] for q in range(4)]
        sums[32 + 8 * k : 40 + 8 * k, :] = jnp.concatenate(pieces, 1)
    rest = jnp.zeros((1, 64), jnp.float32)
    sums[56:57, :] = jnp.concatenate([diagonal(blocks[2][2]), diagonal(blocks[2][4]), rest], 1)
    sums[57:64, :] = jnp.zeros((7, LANES), jnp.float32)


def diagonal(block):
    here = lanes((32, 32)) == lax.broadcasted_iota(jnp.int32, (32, 32), 0)
    return jnp.sum(jnp.where(here, block, 0.0), 0, keepdims=True)


def parted(mixed, ends):
    turned = mixed.T
    lane = lanes((32, 32))
    row = lax.broadcasted_iota(jnp.int32, (32, 32), 0)
    upper = jnp.where(lane > row, mixed, turned)
    return jnp.where(lane <= row, mixed, turned), jnp.where(lane == row, ends, upper)


def eliminate(slabs):
    slabs = list(slabs)
    count = len(slabs)
    tile = (8, LANES)
    lane = lanes(tile)
    row = lax.broadcasted_iota(jnp.int32, tile, 0)

    def spread(slab, column):
        return jnp.broadcast_to(slabs[slab][:, column : column + 1], tile)

    ahead = [spread(0, k) for k in range(8)]
    for g in range(count):
        cols = [[ahead[k]] + [spread(i, 8 * g + k) for i in range(g + 1, count)] for k in range(8)]
        ahead = [spread(g + 1, 8 * g + 8 + k) for k in range(8)] if g + 1 < count else []
        for k in range(8):
            here = lane == 8 * g + k
            root = lax.rsqrt(cols[k][0][k : k + 1, :])
            inverse = root * root
            pivot_row = jnp.where(here[:1], 1.0, slabs[g][k : k + 1, :])
            scaled = pivot_row * inverse
            later = [cols[m][0][k : k + 1, :] * inverse for m in range(k + 1, 8)]
            for i in range(count - g):
                factor = cols[k][i]
                if i == 0:
                    factor = jnp.where(row > k, factor, 0.0)
                    kept = jnp.where(here & (row > k), 0.0, slabs[g])
                    slabs[g] = jnp.where(row == k, pivot_row * root, kept - factor * scaled)
                else:
                    slabs[g + i] = jnp.where(here, 0.0, slabs[g + i]) - factor * scaled
                for m in range(k + 1, 8):
                    cols[m][i] = cols[m][i] - factor * later[m - k - 1]
            if ahead:
                below = cols[k][1]
                ahead = [ahead[c] - below * (below[c : c + 1, :] * inverse) for c in range(8)]
    return slabs


def lower_part(slabs, size):
    whole = jnp.concatenate(slabs, 0)
    row = lax.broadcasted_iota(jnp.int32, whole.shape, 0)
    return jnp.where(lanes(whole.shape) <= row, whole, 0.0)[:, :size]


def update(scale, sums, start, fields, new_basis, new_search, values):
    first = sums[0:32, :] * scale
    second = sums[32:64, :] * scale
    mixed, xy, xp, pz = (first[:, 32 * k : 32 * k + 32] for k in range(4))
    other, yp, yz = (
        jnp.concatenate([second[8 * k : 8 * k + 8, 32 * q : 32 * q + 32] for q in range(4)], 0)
        for k in range(3)
    )
    xx, pp = parted(mixed, second[24:25, 0:32])
    yy, pr = parted(other, second[24:25, 32:64])
    px, py, zp = xp.T, yp.T, pz.T
    zero = jnp.zeros((32, 32), jnp.float32)
    gram = [
        jnp.concatenate([xx, xy, xp, zero], 1),
        jnp.concatenate([xy, yy, yp, zero], 1),
        jnp.concatenate([px, py, pp, zero], 1),
    ]
    projected = jnp.concatenate(
        [
            jnp.concatenate([xy, yy, yp], 1),
            jnp.concatenate([yy, yz, zp], 1),
            jnp.concatenate([py, pz, pr], 1),
        ],
        0,
    )
    lower_inv = lower_part(
        eliminate([block[8 * k : 8 * k + 8] for block in gram for k in range(4)]), 96
    )
    half = dot_nn(lower_inv, projected)
    ritz = 0.5 * (dot_nt(half, lower_inv) + dot_nt(lower_inv, half))
    bound = jnp.max(jnp.sum(jnp.abs(ritz), 0, keepdims=True), 1, keepdims=True)
    seed = start[...].astype(jnp.float32)
    moved = bound * seed - dot_nn(seed, ritz)
    square = jnp.concatenate([dot_nt(moved, moved), jnp.zeros((32, 96), jnp.float32)], 1)
    weights = dot_nn(moved, lower_inv)
    quotient = diagonal(xy) / diagonal(xx)
    middle = weights[:, 32:64]
    search_weights = jnp.concatenate([-(middle * quotient), middle, weights[:, 64:96]], 1)
    mixed_fields = dot_nn(jnp.concatenate([weights, search_weights], 0), fields[...])
    mixed_ritz = dot_nn(moved, ritz)
    small_inv = lower_part(eliminate([square[8 * k : 8 * k + 8] for k in range(4)]), 32)
    both = jnp.concatenate([mixed_fields[0:32], mixed_fields[32:64]], 1)
    result = dot_nn(small_inv, both)
    terms = dot_nn(small_inv, moved) * dot_nn(small_inv, mixed_ritz)
    values[...] = dot_nt(jnp.ones((8, 96), jnp.float32), terms)[0:1, :]
    wide = ROWS * LANES
    for s in range(ROWS):
        new_basis[:, s, :] = result[:, LANES * s : LANES * (s + 1)]
        new_search[:, s, :] = result[:, wide + LANES * s : wide + LANES * (s + 1)]


def call(kernel, outs, *args, scratch=(), place=VMEM, cost=None):
    shapes = [jax.ShapeDtypeStruct(shape, jnp.float32) for shape in outs]
    return pl.pallas_call(
        kernel,
        out_shape=shapes,
        in_specs=[place] * len(args),
        cost_estimate=cost,
        out_specs=[VMEM] * len(shapes),
        scratch_shapes=[
            pltpu.VMEM(shape, jnp.float32) if isinstance(shape, tuple) else shape for shape in scratch
        ],
        compiler_params=pltpu.CompilerParams(vmem_limit_bytes=32 * 1024 * 1024),
    )(*args)


def paired(array, axis, first):
    pairs = [(i, i + 1) for i in range(first, lax.axis_size(axis) - 1, 2)]
    return lax.ppermute(array, axis, pairs + [(j, i) for i, j in pairs])


def exchanged(array, axis):
    return lax.all_to_all(array, axis, 0, 0, tiled=True)


def summed(array, count):
    return jnp.sum(array.reshape(count, array.shape[0] // count, LANES), 0)


def total(array):
    across, along = lax.axis_size("gy"), lax.axis_size("gx")
    share = summed(exchanged(array, "gy"), across)
    share = summed(exchanged(jnp.tile(share, (along, 1)), "gx"), along)
    return exchanged(jnp.tile(share, (across, 1)), "gy")


def body(basis, search, conductivity, rotation):
    modes, cells_x, flat = basis.shape
    count = cells_x * flat * lax.axis_size("gx") * lax.axis_size("gy")
    blocks = [basis.shape, search.shape, conductivity.shape]
    rows = call(
        pack_rows,
        [(104, LANES)] * 2,
        *(pltpu.with_memory_space_constraint(x, pltpu.HBM) for x in (basis, search, conductivity)),
        scratch=blocks + [pltpu.SemaphoreType.DMA((3,))],
        place=pl.BlockSpec(memory_space=pltpu.HBM),
    )
    inner_x, inner_p = call(
        inner,
        [(cells_x, modes, flat)] * 2,
        basis,
        search,
        conductivity,
        scratch=[(4, ROWS, LANES)],
        cost=pl.CostEstimate(flops=4 << 20, bytes_accessed=1 << 20, transcendentals=0),
    )
    row_two = paired(rows[1], "gx", 1)
    row_one = paired(rows[0], "gx", 0)
    side_one, side_two, lo, hi = call(
        pack_sides,
        [(112, LANES)] * 2 + [(104, LANES)] * 2,
        basis,
        search,
        conductivity,
        row_two,
        row_one,
        scratch=[(112, LANES)] * 2,
    )
    side_two = paired(side_two, "gy", 1)
    side_one = paired(side_one, "gy", 0)
    fields, sums = call(
        images,
        [(96, ROWS * LANES), (64, LANES)],
        basis,
        search,
        conductivity,
        inner_x,
        inner_p,
        lo,
        hi,
        side_two,
        side_one,
        scratch=[(2, 24, LANES), (2, 5, 16, LANES), (2, 10, MODES, LANES), (160, ROWS * LANES)]
        + [(112, LANES)] * 2,
    )
    sums = total(sums)

    def finish(*refs):
        update(1.0 / count, *refs)

    new_basis, new_search, values = call(
        finish,
        [(modes, cells_x, flat), (modes, cells_x, flat), (1, modes)],
        sums,
        rotation.T,
        fields,
    )
    return new_basis, new_search, values.reshape(modes)


def solution(mesh):
    in_specs = (P(None, "gx", "gy"), P(None, "gx", "gy"), P("gx", "gy"), P())
    out_specs = (P(None, "gx", "gy"), P(None, "gx", "gy"), P())
    return jax.shard_map(body, mesh=mesh, in_specs=in_specs, out_specs=out_specs, check_vma=False)
```

```python
import jax
import jax.numpy as jnp
from jax import lax
from jax.experimental import pallas as pl
from jax.experimental.pallas import tpu as pltpu
from jax.sharding import PartitionSpec as P

CZ = 16
MODES = 32
ROWS = 8
LANES = 128
HIGH = lax.Precision.HIGHEST
VMEM = pl.BlockSpec(memory_space=pltpu.VMEM)


def dot_nt(left, right):
    return lax.dot_general(
        left, right, (((1,), (1,)), ((), ())), precision=HIGH, preferred_element_type=jnp.float32
    )


def dot_nn(left, right):
    return lax.dot_general(
        left, right, (((1,), (0,)), ((), ())), precision=HIGH, preferred_element_type=jnp.float32
    )


def roll(array, shift):
    shift = shift % LANES
    return pltpu.roll(array, shift, array.ndim - 1) if shift else array


def lanes(shape):
    return lax.broadcasted_iota(jnp.int32, shape, len(shape) - 1)


def is_odd(axis):
    return lax.axis_index(axis) % 2 == 1


def sort_sides(axis, one, two, low, high):
    odd = is_odd(axis)
    low[...] = jnp.where(odd, one[...], two[...])
    high[...] = jnp.where(odd, two[...], one[...])


def pack_rows(basis_hbm, search_hbm, cond_hbm, one, two, basis, search, cond, arrived):
    copies = [
        pltpu.make_async_copy(source, target, arrived.at[k])
        for k, (source, target) in enumerate(
            ((basis_hbm, basis), (search_hbm, search), (cond_hbm, cond))
        )
    ]
    for copy in copies:
        copy.start()
    for copy in copies:
        copy.wait()
    up = [basis[:, 6, :], basis[:, 7, :], search[:, 7, :]]
    down = [basis[:, 0, :], basis[:, 1, :], search[:, 0, :]]
    odd = is_odd("gx")
    for k in range(3):
        one[32 * k : 32 * k + 32, :] = jnp.where(odd, down[k], up[k])
        two[32 * k : 32 * k + 32, :] = jnp.where(odd, up[k], down[k])
    one[96:104, :] = cond[...]
    two[96:104, :] = cond[...]


def pack_layers(rows, right):
    lane = lanes(rows[0].shape) // CZ
    outer = second = None
    for s in range(ROWS):
        moved = roll(rows[s], CZ * (s + 1 if right else s))
        at = (s - 1 if right else s + 1) % ROWS
        outer = moved if outer is None else jnp.where(lane == s, moved, outer)
        second = moved if second is None else jnp.where(lane == at, moved, second)
    return outer, second


def pack_ends(before, after, right):
    before = roll(before, CZ if right else 0)
    after = roll(after, 2 * CZ if right else CZ)
    return jnp.where(lanes(before.shape) < CZ, before, after)


def pack_sides(basis, search, cond, row_two, row_one, side_one, side_two, lo, hi, right, left):
    sort_sides("gx", row_one, row_two, lo, hi)
    block = (8, LANES)
    field = [basis[:, s, :] for s in range(ROWS)]
    other = [search[:, s, :] for s in range(ROWS)]
    cells = [jnp.broadcast_to(cond[s : s + 1, :], block) for s in range(ROWS)]
    cell_lo = jnp.broadcast_to(lo[103:104, :], block)
    cell_hi = jnp.broadcast_to(hi[96:97, :], block)
    lane = lanes(block)
    for message, to_right in ((right, True), (left, False)):
        message[0:32, :], message[32:64, :] = pack_layers(field, to_right)
        message[64:96, :] = pack_layers(other, to_right)[0]
        ends = pack_ends(lo[32:64, :], hi[0:32, :], to_right)
        folded = ends[0:8]
        for q in range(1, 4):
            folded = jnp.where(lane >= 32 * q, roll(ends[8 * q : 8 * q + 8], 32 * q), folded)
        message[96:104, :] = folded
        cell_outer, cell_second = pack_layers(cells, to_right)
        message[104:105, :] = cell_outer[:1]
        message[105:106, :] = cell_second[:1]
        message[106:107, :] = pack_ends(cell_lo, cell_hi, to_right)[:1]
        message[107:112, :] = jnp.zeros((5, LANES), jnp.float32)
    sort_sides("gy", left, right, side_one, side_two)


def side_tile(low, high, s):
    lane = lanes(low[0].shape) // CZ
    if 0 <= s < ROWS:
        above = [roll(part, -CZ * s) for part in high[:2]]
        below = [roll(part, CZ * (7 - s)) for part in low[:2]]
        tile = jnp.where(lane == 0, above[0], jnp.where(lane == 7, below[0], 0.0))
        if len(above) == 2:
            tile = jnp.where(lane == 1, above[1], jnp.where(lane == 6, below[1], tile))
        return tile
    k = 0 if s < 0 else 1
    above, below = roll(high[2], -CZ * k), roll(low[2], CZ * (7 - k))
    return jnp.where(lane == 0, above, jnp.where(lane == 7, below, 0.0))


def unfolded(folded):
    return jnp.concatenate([roll(folded, -32 * q) for q in range(4)], 0)


def next_y(own, side):
    lane = lanes(own.shape)
    a, b = roll(own, -CZ), roll(side, -CZ)
    return jnp.where(lane < LANES - CZ, a, b), jnp.where(lane < LANES - CZ, b, a)


def prev_y(own, side):
    lane = lanes(own.shape)
    a, b = roll(own, CZ), roll(side, CZ)
    return jnp.where(lane >= CZ, a, b), jnp.where(lane >= CZ, b, a)


def next_z(array):
    return jnp.where(lanes(array.shape) % CZ == CZ - 1, roll(array, CZ - 1), roll(array, -1))


def prev_z(array):
    return jnp.where(lanes(array.shape) % CZ == 0, roll(array, 1 - CZ), roll(array, 1))


def inner(basis, search, cond, image, other, coef):
    lane = lanes((ROWS, LANES))
    cells = cond[...]
    after, before = roll(cells, -CZ), roll(cells, CZ)
    coef[0] = jnp.where(lane < LANES - CZ, 0.5 * (cells + after), 0.0)
    coef[1] = jnp.where(lane >= CZ, 0.5 * (cells + before), 0.0)
    coef[2] = 0.5 * (cells + next_z(cells))
    coef[3] = 0.5 * (cells + prev_z(cells))
    for field, result in ((basis, image), (search, other)):
        flux = None
        for s in range(ROWS):
            own = field[:, s, :]
            total = coef[0, s : s + 1, :] * (own - roll(own, -CZ))
            total += coef[1, s : s + 1, :] * (own - roll(own, CZ))
            total += coef[2, s : s + 1, :] * (own - next_z(own))
            total += coef[3, s : s + 1, :] * (own - prev_z(own))
            if s > 0:
                total += flux
            if s < ROWS - 1:
                face = 0.5 * (cond[s : s + 1, :] + cond[s + 1 : s + 2, :])
                flux = face * (field[:, s + 1, :] - own)
                total -= flux
            result[s] = total


def images(
    basis, search, cond, inner_x, inner_p, lo, hi, side_two, side_one, fields, sums, conds, coef, image, stack, low, high
):
    sort_sides("gy", side_one, side_two, low, high)
    basis_sides = [(part[0:32, :], part[32:64, :], unfolded(part[96:104, :])) for part in (low, high)]
    search_sides = [(part[64:96, :],) for part in (low, high)]
    cond_sides = [
        [jnp.broadcast_to(part[r : r + 1, :], (8, LANES)) for r in range(104, 107)] for part in (low, high)
    ]
    conds[...] = jnp.zeros_like(conds)
    conds[0, 0:2, :] = lo[102:104, :]
    conds[0, 2:10, :] = cond[...]
    conds[0, 10:12, :] = hi[96:98, :]
    for r in range(10):
        conds[1, r + 1 : r + 2, :] = side_tile(*cond_sides, r - 1)[:1]
    cond_a, cond_b = conds[0, 0:16, :], conds[1, 0:16, :]
    after = next_y(cond_a, cond_b)
    before = prev_y(cond_a, cond_b)
    for part, array in ((0, cond_a), (1, cond_b)):
        coef[part, 0] = 0.5 * (array + conds[part, 1:17, :])
        coef[part, 1] = 0.5 * (array + after[part])
        coef[part, 2] = 0.5 * (array + before[part])
        coef[part, 3] = 0.5 * (array + next_z(array))
        coef[part, 4] = 0.5 * (array + prev_z(array))

    def operator(part, r, own, beside, x_low, x_high):
        i = r + 2
        total = coef[part, 0, i - 1 : i, :] * (own - x_low)
        total += coef[part, 0, i : i + 1, :] * (own - x_high)
        total += coef[part, 1, i : i + 1, :] * (own - beside[0])
        total += coef[part, 2, i : i + 1, :] * (own - beside[1])
        total += coef[part, 3, i : i + 1, :] * (own - next_z(own))
        total += coef[part, 4, i : i + 1, :] * (own - prev_z(own))
        return total

    def outer(s, own, side, x_low, x_high):
        i = s + 2
        group = lanes(own.shape) // CZ
        other = jnp.where(group == 0, roll(side, CZ), roll(side, -CZ))
        first = lanes((1, LANES)) // CZ
        face = jnp.where(first == 0, coef[0, 2, i : i + 1, :], 0.0)
        face = jnp.where(first == 7, coef[0, 1, i : i + 1, :], face)
        total = face * (own - other)
        if s == 0:
            total += coef[0, 0, i - 1 : i, :] * (own - x_low)
        if s == ROWS - 1:
            total += coef[0, 0, i : i + 1, :] * (own - x_high)
        return total

    def beside(own, side):
        after, before = next_y(own, side), prev_y(own, side)
        return ((after[0], before[0]), (after[1], before[1]))

    def basis_row(r):
        if r < 0:
            return lo[32 * (r + 2) : 32 * (r + 3), :]
        if r >= ROWS:
            return hi[32 * (r - ROWS) : 32 * (r - ROWS + 1), :]
        return basis[:, r, :]

    def valid(part, r, array):
        return jnp.where(conds[part, r + 2 : r + 3, :] > 0.0, array, 0.0)

    sides = {r: side_tile(*basis_sides, r) for r in range(-1, 2)}
    for r in range(-1, ROWS + 1):
        if 1 <= r < ROWS:
            sides[r + 1] = side_tile(*basis_sides, r + 1)
        own = basis_row(r)
        pairs = beside(own, sides[r])
        if 0 <= r < ROWS:
            image[0, r + 1] = inner_x[r] + outer(r, own, sides[r], basis_row(-1), basis_row(ROWS))
        else:
            first = operator(0, r, own, pairs[0], basis_row(r - 1), basis_row(r + 1))
            image[0, r + 1] = valid(0, r, first)
        if 0 <= r < ROWS:
            second = operator(1, r, sides[r], pairs[1], sides[r - 1], sides[r + 1])
            image[1, r + 1] = valid(1, r, second)

    for s in range(ROWS):
        at = slice(LANES * s, LANES * (s + 1))
        field = search[:, s, :]
        side = side_tile(*search_sides, s)
        stack[128:160, at] = inner_p[s] + outer(s, field, side, lo[64:96, :], hi[64:96, :])
        own = image[0, s + 1]
        pairs = beside(own, image[1, s + 1])
        stack[96:128, at] = operator(0, s, own, pairs[0], image[0, s], image[0, s + 2])
        stack[0:32, at] = basis[:, s, :]
        stack[32:64, at] = own
        stack[64:96, at] = field
        fields[0:32, at] = basis[:, s, :]
        fields[32:64, at] = own
        fields[64:96, at] = field

    product = dot_nt(stack[0:96, :], stack[...])
    blocks = [[product[32 * i : 32 * i + 32, 32 * j : 32 * j + 32] for j in range(5)] for i in range(3)]
    lower = lanes((32, 32)) <= lax.broadcasted_iota(jnp.int32, (32, 32), 0)
    first = jnp.where(lower, blocks[0][0], blocks[2][2])
    second = jnp.where(lower, blocks[1][1], blocks[2][4])
    sums[0:32, :] = jnp.concatenate([first, blocks[0][1], blocks[0][2], blocks[2][3]], 1)
    for k, block in enumerate((second, blocks[1][2], blocks[1][3])):
        pieces = [block[8 * q : 8 * q + 8] for q in range(4)]
        sums[32 + 8 * k : 40 + 8 * k, :] = jnp.concatenate(pieces, 1)
    rest = jnp.zeros((1, 64), jnp.float32)
    sums[56:57, :] = jnp.concatenate([diagonal(blocks[2][2]), diagonal(blocks[2][4]), rest], 1)
    sums[57:64, :] = jnp.zeros((7, LANES), jnp.float32)


def diagonal(block):
    here = lanes((32, 32)) == lax.broadcasted_iota(jnp.int32, (32, 32), 0)
    return jnp.sum(jnp.where(here, block, 0.0), 0, keepdims=True)


def parted(mixed, ends):
    turned = mixed.T
    lane = lanes((32, 32))
    row = lax.broadcasted_iota(jnp.int32, (32, 32), 0)
    upper = jnp.where(lane > row, mixed, turned)
    return jnp.where(lane <= row, mixed, turned), jnp.where(lane == row, ends, upper)


def eliminate(slabs):
    slabs = list(slabs)
    count = len(slabs)
    tile = (8, LANES)
    lane = lanes(tile)
    row = lax.broadcasted_iota(jnp.int32, tile, 0)

    def spread(slab, column):
        return jnp.broadcast_to(slabs[slab][:, column : column + 1], tile)

    ahead = [spread(0, k) for k in range(8)]
    for g in range(count):
        cols = [[ahead[k]] + [spread(i, 8 * g + k) for i in range(g + 1, count)] for k in range(8)]
        ahead = [spread(g + 1, 8 * g + 8 + k) for k in range(8)] if g + 1 < count else []
        for k in range(8):
            here = lane == 8 * g + k
            root = lax.rsqrt(jnp.broadcast_to(cols[k][0][k : k + 1, :], tile))
            inverse = root * root
            pivot_row = jnp.where(here, 1.0, jnp.broadcast_to(slabs[g][k : k + 1, :], tile))
            scaled = pivot_row * inverse
            entries = [jnp.broadcast_to(cols[m][0][k : k + 1, :], tile) for m in range(k + 1, 8)]
            later = [entry * inverse for entry in entries]
            for i in range(count - g):
                factor = cols[k][i]
                if i == 0:
                    factor = jnp.where(row > k, factor, 0.0)
                    kept = jnp.where(here & (row > k), 0.0, slabs[g])
                    slabs[g] = jnp.where(row == k, pivot_row * root, kept - factor * scaled)
                else:
                    slabs[g + i] = jnp.where(here, 0.0, slabs[g + i]) - factor * scaled
                for m in range(k + 1, 8):
                    if i == 0:
                        cols[m][i] = cols[m][i] - (factor * entries[m - k - 1]) * inverse
                    else:
                        cols[m][i] = cols[m][i] - factor * later[m - k - 1]
            if ahead:
                below = cols[k][1]
                ahead = [ahead[c] - (below * below[c : c + 1, :]) * inverse for c in range(8)]
    return slabs


def lower_part(slabs, size):
    whole = jnp.concatenate(slabs, 0)
    row = lax.broadcasted_iota(jnp.int32, whole.shape, 0)
    return jnp.where(lanes(whole.shape) <= row, whole, 0.0)[:, :size]


def update(scale, sums, start, fields, new_basis, new_search, values):
    first = sums[0:32, :] * scale
    second = sums[32:64, :] * scale
    mixed, xy, xp, pz = (first[:, 32 * k : 32 * k + 32] for k in range(4))
    other, yp, yz = (
        jnp.concatenate([second[8 * k : 8 * k + 8, 32 * q : 32 * q + 32] for q in range(4)], 0)
        for k in range(3)
    )
    xx, pp = parted(mixed, second[24:25, 0:32])
    yy, pr = parted(other, second[24:25, 32:64])
    px, py, zp = xp.T, yp.T, pz.T
    zero = jnp.zeros((32, 32), jnp.float32)
    gram = [
        jnp.concatenate([xx, xy, xp, zero], 1),
        jnp.concatenate([xy, yy, yp, zero], 1),
        jnp.concatenate([px, py, pp, zero], 1),
    ]
    projected = jnp.concatenate(
        [
            jnp.concatenate([xy, yy, yp], 1),
            jnp.concatenate([yy, yz, zp], 1),
            jnp.concatenate([py, pz, pr], 1),
        ],
        0,
    )
    lower_inv = lower_part(
        eliminate([block[8 * k : 8 * k + 8] for block in gram for k in range(4)]), 96
    )
    half = dot_nn(lower_inv, projected)
    ritz = 0.5 * (dot_nt(half, lower_inv) + dot_nt(lower_inv, half))
    bound = jnp.max(jnp.sum(jnp.abs(ritz), 0, keepdims=True), 1, keepdims=True)
    seed = start[...].astype(jnp.float32)
    moved = bound * seed - dot_nn(seed, ritz)
    square = jnp.concatenate([dot_nt(moved, moved), jnp.zeros((32, 96), jnp.float32)], 1)
    weights = dot_nn(moved, lower_inv)
    quotient = diagonal(xy) / diagonal(xx)
    middle = weights[:, 32:64]
    search_weights = jnp.concatenate([-(middle * quotient), middle, weights[:, 64:96]], 1)
    mixed_fields = dot_nn(jnp.concatenate([weights, search_weights], 0), fields[...])
    mixed_ritz = dot_nn(moved, ritz)
    small_inv = lower_part(eliminate([square[8 * k : 8 * k + 8] for k in range(4)]), 32)
    both = jnp.concatenate([mixed_fields[0:32], mixed_fields[32:64]], 1)
    result = dot_nn(small_inv, both)
    terms = dot_nn(small_inv, moved) * dot_nn(small_inv, mixed_ritz)
    values[...] = dot_nt(jnp.ones((8, 96), jnp.float32), terms)[0:1, :]
    wide = ROWS * LANES
    for s in range(ROWS):
        new_basis[:, s, :] = result[:, LANES * s : LANES * (s + 1)]
        new_search[:, s, :] = result[:, wide + LANES * s : wide + LANES * (s + 1)]


def call(kernel, outs, *args, scratch=(), place=VMEM, cost=None):
    shapes = [jax.ShapeDtypeStruct(shape, jnp.float32) for shape in outs]
    return pl.pallas_call(
        kernel,
        out_shape=shapes,
        in_specs=[place] * len(args),
        cost_estimate=cost,
        out_specs=[VMEM] * len(shapes),
        scratch_shapes=[
            pltpu.VMEM(shape, jnp.float32) if isinstance(shape, tuple) else shape for shape in scratch
        ],
        compiler_params=pltpu.CompilerParams(vmem_limit_bytes=32 * 1024 * 1024),
    )(*args)


def paired(array, axis, first):
    pairs = [(i, i + 1) for i in range(first, lax.axis_size(axis) - 1, 2)]
    return lax.ppermute(array, axis, pairs + [(j, i) for i, j in pairs])


def exchanged(array, axis):
    return lax.all_to_all(array, axis, 0, 0, tiled=True)


def summed(array, count):
    return jnp.sum(array.reshape(count, array.shape[0] // count, LANES), 0)


def total(array):
    across, along = lax.axis_size("gy"), lax.axis_size("gx")
    share = summed(exchanged(array, "gy"), across)
    share = summed(exchanged(jnp.tile(share, (along, 1)), "gx"), along)
    return exchanged(jnp.tile(share, (across, 1)), "gy")


def body(basis, search, conductivity, rotation):
    modes, cells_x, flat = basis.shape
    count = cells_x * flat * lax.axis_size("gx") * lax.axis_size("gy")
    blocks = [basis.shape, search.shape, conductivity.shape]
    rows = call(
        pack_rows,
        [(104, LANES)] * 2,
        *(pltpu.with_memory_space_constraint(x, pltpu.HBM) for x in (basis, search, conductivity)),
        scratch=blocks + [pltpu.SemaphoreType.DMA((3,))],
        place=pl.BlockSpec(memory_space=pltpu.HBM),
    )
    inner_x, inner_p = call(
        inner,
        [(cells_x, modes, flat)] * 2,
        basis,
        search,
        conductivity,
        scratch=[(4, ROWS, LANES)],
        cost=pl.CostEstimate(flops=4 << 20, bytes_accessed=1 << 20, transcendentals=0),
    )
    row_two = paired(rows[1], "gx", 1)
    row_one = paired(rows[0], "gx", 0)
    side_one, side_two, lo, hi = call(
        pack_sides,
        [(112, LANES)] * 2 + [(104, LANES)] * 2,
        basis,
        search,
        conductivity,
        row_two,
        row_one,
        scratch=[(112, LANES)] * 2,
    )
    side_two = paired(side_two, "gy", 1)
    side_one = paired(side_one, "gy", 0)
    fields, sums = call(
        images,
        [(96, ROWS * LANES), (64, LANES)],
        basis,
        search,
        conductivity,
        inner_x,
        inner_p,
        lo,
        hi,
        side_two,
        side_one,
        scratch=[(2, 24, LANES), (2, 5, 16, LANES), (2, 10, MODES, LANES), (160, ROWS * LANES)]
        + [(112, LANES)] * 2,
    )
    sums = total(sums)

    def finish(*refs):
        update(1.0 / count, *refs)

    new_basis, new_search, values = call(
        finish,
        [(modes, cells_x, flat), (modes, cells_x, flat), (1, modes)],
        sums,
        rotation.T,
        fields,
    )
    return new_basis, new_search, values.reshape(modes)


def solution(mesh):
    in_specs = (P(None, "gx", "gy"), P(None, "gx", "gy"), P("gx", "gy"), P())
    out_specs = (P(None, "gx", "gy"), P(None, "gx", "gy"), P())
    return jax.shard_map(body, mesh=mesh, in_specs=in_specs, out_specs=out_specs, check_vma=False)
```

```python
import jax
import jax.numpy as jnp
from jax import lax
from jax.experimental import pallas as pl
from jax.experimental.pallas import tpu as pltpu
from jax.sharding import PartitionSpec as P

CZ = 16
MODES = 32
ROWS = 8
LANES = 128
HIGH = lax.Precision.HIGHEST
VMEM = pl.BlockSpec(memory_space=pltpu.VMEM)


def dot_nt(left, right):
    return lax.dot_general(
        left, right, (((1,), (1,)), ((), ())), precision=HIGH, preferred_element_type=jnp.float32
    )


def dot_nn(left, right):
    return lax.dot_general(
        left, right, (((1,), (0,)), ((), ())), precision=HIGH, preferred_element_type=jnp.float32
    )


def roll(array, shift):
    shift = shift % LANES
    return pltpu.roll(array, shift, array.ndim - 1) if shift else array


def lanes(shape):
    return lax.broadcasted_iota(jnp.int32, shape, len(shape) - 1)


def is_odd(axis):
    return lax.axis_index(axis) % 2 == 1


def sort_sides(axis, one, two, low, high):
    odd = is_odd(axis)
    low[...] = jnp.where(odd, one[...], two[...])
    high[...] = jnp.where(odd, two[...], one[...])


def pack_rows(basis_hbm, search_hbm, cond_hbm, one, two, basis, search, cond, arrived):
    copies = [
        pltpu.make_async_copy(source, target, arrived.at[k])
        for k, (source, target) in enumerate(
            ((basis_hbm, basis), (search_hbm, search), (cond_hbm, cond))
        )
    ]
    for copy in copies:
        copy.start()
    for copy in copies:
        copy.wait()
    up = [basis[:, 6, :], basis[:, 7, :], search[:, 7, :]]
    down = [basis[:, 0, :], basis[:, 1, :], search[:, 0, :]]
    odd = is_odd("gx")
    for k in range(3):
        one[32 * k : 32 * k + 32, :] = jnp.where(odd, down[k], up[k])
        two[32 * k : 32 * k + 32, :] = jnp.where(odd, up[k], down[k])
    one[96:104, :] = cond[...]
    two[96:104, :] = cond[...]


def pack_layers(rows, right):
    lane = lanes(rows[0].shape) // CZ
    outer = second = None
    for s in range(ROWS):
        moved = roll(rows[s], CZ * (s + 1 if right else s))
        at = (s - 1 if right else s + 1) % ROWS
        outer = moved if outer is None else jnp.where(lane == s, moved, outer)
        second = moved if second is None else jnp.where(lane == at, moved, second)
    return outer, second


def pack_ends(before, after, right):
    before = roll(before, CZ if right else 0)
    after = roll(after, 2 * CZ if right else CZ)
    return jnp.where(lanes(before.shape) < CZ, before, after)


def pack_sides(basis, search, cond, row_two, row_one, side_one, side_two, lo, hi, right, left):
    sort_sides("gx", row_one, row_two, lo, hi)
    block = (8, LANES)
    field = [basis[:, s, :] for s in range(ROWS)]
    other = [search[:, s, :] for s in range(ROWS)]
    cells = [jnp.broadcast_to(cond[s : s + 1, :], block) for s in range(ROWS)]
    cell_lo = jnp.broadcast_to(lo[103:104, :], block)
    cell_hi = jnp.broadcast_to(hi[96:97, :], block)
    lane = lanes(block)
    for message, to_right in ((right, True), (left, False)):
        message[0:32, :], message[32:64, :] = pack_layers(field, to_right)
        message[64:96, :] = pack_layers(other, to_right)[0]
        ends = pack_ends(lo[32:64, :], hi[0:32, :], to_right)
        folded = ends[0:8]
        for q in range(1, 4):
            folded = jnp.where(lane >= 32 * q, roll(ends[8 * q : 8 * q + 8], 32 * q), folded)
        message[96:104, :] = folded
        cell_outer, cell_second = pack_layers(cells, to_right)
        message[104:105, :] = cell_outer[:1]
        message[105:106, :] = cell_second[:1]
        message[106:107, :] = pack_ends(cell_lo, cell_hi, to_right)[:1]
        message[107:112, :] = jnp.zeros((5, LANES), jnp.float32)
    sort_sides("gy", left, right, side_one, side_two)


def side_tile(low, high, s):
    lane = lanes(low[0].shape) // CZ
    if 0 <= s < ROWS:
        above = [roll(part, -CZ * s) for part in high[:2]]
        below = [roll(part, CZ * (7 - s)) for part in low[:2]]
        tile = jnp.where(lane == 0, above[0], jnp.where(lane == 7, below[0], 0.0))
        if len(above) == 2:
            tile = jnp.where(lane == 1, above[1], jnp.where(lane == 6, below[1], tile))
        return tile
    k = 0 if s < 0 else 1
    above, below = roll(high[2], -CZ * k), roll(low[2], CZ * (7 - k))
    return jnp.where(lane == 0, above, jnp.where(lane == 7, below, 0.0))


def unfolded(folded):
    return jnp.concatenate([roll(folded, -32 * q) for q in range(4)], 0)


def next_y(own, side):
    lane = lanes(own.shape)
    a, b = roll(own, -CZ), roll(side, -CZ)
    return jnp.where(lane < LANES - CZ, a, b), jnp.where(lane < LANES - CZ, b, a)


def prev_y(own, side):
    lane = lanes(own.shape)
    a, b = roll(own, CZ), roll(side, CZ)
    return jnp.where(lane >= CZ, a, b), jnp.where(lane >= CZ, b, a)


def next_z(array):
    return jnp.where(lanes(array.shape) % CZ == CZ - 1, roll(array, CZ - 1), roll(array, -1))


def prev_z(array):
    return jnp.where(lanes(array.shape) % CZ == 0, roll(array, 1 - CZ), roll(array, 1))


def inner(basis, search, cond, image, other, coef):
    lane = lanes((ROWS, LANES))
    cells = cond[...]
    after, before = roll(cells, -CZ), roll(cells, CZ)
    coef[0] = jnp.where(lane < LANES - CZ, 0.5 * (cells + after), 0.0)
    coef[1] = jnp.where(lane >= CZ, 0.5 * (cells + before), 0.0)
    coef[2] = 0.5 * (cells + next_z(cells))
    coef[3] = 0.5 * (cells + prev_z(cells))
    for field, result in ((basis, image), (search, other)):
        flux = None
        for s in range(ROWS):
            own = field[:, s, :]
            total = coef[0, s : s + 1, :] * (own - roll(own, -CZ))
            total += coef[1, s : s + 1, :] * (own - roll(own, CZ))
            total += coef[2, s : s + 1, :] * (own - next_z(own))
            total += coef[3, s : s + 1, :] * (own - prev_z(own))
            if s > 0:
                total += flux
            if s < ROWS - 1:
                face = 0.5 * (cond[s : s + 1, :] + cond[s + 1 : s + 2, :])
                flux = face * (field[:, s + 1, :] - own)
                total -= flux
            result[s] = total


def images(
    basis, search, cond, inner_x, inner_p, lo, hi, side_two, side_one, fields, sums, conds, coef, image, stack, low, high
):
    sort_sides("gy", side_one, side_two, low, high)
    basis_sides = [(part[0:32, :], part[32:64, :], unfolded(part[96:104, :])) for part in (low, high)]
    search_sides = [(part[64:96, :],) for part in (low, high)]
    cond_sides = [
        [jnp.broadcast_to(part[r : r + 1, :], (8, LANES)) for r in range(104, 107)] for part in (low, high)
    ]
    conds[...] = jnp.zeros_like(conds)
    conds[0, 0:2, :] = lo[102:104, :]
    conds[0, 2:10, :] = cond[...]
    conds[0, 10:12, :] = hi[96:98, :]
    for r in range(10):
        conds[1, r + 1 : r + 2, :] = side_tile(*cond_sides, r - 1)[:1]
    cond_a, cond_b = conds[0, 0:16, :], conds[1, 0:16, :]
    after = next_y(cond_a, cond_b)
    before = prev_y(cond_a, cond_b)
    for part, array in ((0, cond_a), (1, cond_b)):
        coef[part, 0] = 0.5 * (array + conds[part, 1:17, :])
        coef[part, 1] = 0.5 * (array + after[part])
        coef[part, 2] = 0.5 * (array + before[part])
        coef[part, 3] = 0.5 * (array + next_z(array))
        coef[part, 4] = 0.5 * (array + prev_z(array))

    def operator(part, r, own, beside, x_low, x_high):
        i = r + 2
        total = coef[part, 0, i - 1 : i, :] * (own - x_low)
        total += coef[part, 0, i : i + 1, :] * (own - x_high)
        total += coef[part, 1, i : i + 1, :] * (own - beside[0])
        total += coef[part, 2, i : i + 1, :] * (own - beside[1])
        total += coef[part, 3, i : i + 1, :] * (own - next_z(own))
        total += coef[part, 4, i : i + 1, :] * (own - prev_z(own))
        return total

    def outer(s, own, side, x_low, x_high):
        i = s + 2
        group = lanes(own.shape) // CZ
        other = jnp.where(group == 0, roll(side, CZ), roll(side, -CZ))
        first = lanes((1, LANES)) // CZ
        face = jnp.where(first == 0, coef[0, 2, i : i + 1, :], 0.0)
        face = jnp.where(first == 7, coef[0, 1, i : i + 1, :], face)
        total = face * (own - other)
        if s == 0:
            total += coef[0, 0, i - 1 : i, :] * (own - x_low)
        if s == ROWS - 1:
            total += coef[0, 0, i : i + 1, :] * (own - x_high)
        return total

    def beside(own, side):
        after, before = next_y(own, side), prev_y(own, side)
        return ((after[0], before[0]), (after[1], before[1]))

    def basis_row(r):
        if r < 0:
            return lo[32 * (r + 2) : 32 * (r + 3), :]
        if r >= ROWS:
            return hi[32 * (r - ROWS) : 32 * (r - ROWS + 1), :]
        return basis[:, r, :]

    def valid(part, r, array):
        return jnp.where(conds[part, r + 2 : r + 3, :] > 0.0, array, 0.0)

    sides = {r: side_tile(*basis_sides, r) for r in range(-1, 2)}
    for r in range(-1, ROWS + 1):
        if 1 <= r < ROWS:
            sides[r + 1] = side_tile(*basis_sides, r + 1)
        own = basis_row(r)
        pairs = beside(own, sides[r])
        if 0 <= r < ROWS:
            image[0, r + 1] = inner_x[r] + outer(r, own, sides[r], basis_row(-1), basis_row(ROWS))
        else:
            first = operator(0, r, own, pairs[0], basis_row(r - 1), basis_row(r + 1))
            image[0, r + 1] = valid(0, r, first)
        if 0 <= r < ROWS:
            second = operator(1, r, sides[r], pairs[1], sides[r - 1], sides[r + 1])
            image[1, r + 1] = valid(1, r, second)

    for s in range(ROWS):
        at = slice(LANES * s, LANES * (s + 1))
        field = search[:, s, :]
        side = side_tile(*search_sides, s)
        stack[128:160, at] = inner_p[s] + outer(s, field, side, lo[64:96, :], hi[64:96, :])
        own = image[0, s + 1]
        pairs = beside(own, image[1, s + 1])
        stack[96:128, at] = operator(0, s, own, pairs[0], image[0, s], image[0, s + 2])
        stack[0:32, at] = basis[:, s, :]
        stack[32:64, at] = own
        stack[64:96, at] = field
        fields[0:32, at] = basis[:, s, :]
        fields[32:64, at] = own
        fields[64:96, at] = field

    product = dot_nt(stack[0:96, :], stack[...])
    blocks = [[product[32 * i : 32 * i + 32, 32 * j : 32 * j + 32] for j in range(5)] for i in range(3)]
    lower = lanes((32, 32)) <= lax.broadcasted_iota(jnp.int32, (32, 32), 0)
    first = jnp.where(lower, blocks[0][0], blocks[2][2])
    second = jnp.where(lower, blocks[1][1], blocks[2][4])
    sums[0:32, :] = jnp.concatenate([first, blocks[0][1], blocks[0][2], blocks[2][3]], 1)
    for k, block in enumerate((second, blocks[1][2], blocks[1][3])):
        pieces = [block[8 * q : 8 * q + 8] for q in range(4)]
        sums[32 + 8 * k : 40 + 8 * k, :] = jnp.concatenate(pieces, 1)
    rest = jnp.zeros((1, 64), jnp.float32)
    sums[56:57, :] = jnp.concatenate([diagonal(blocks[2][2]), diagonal(blocks[2][4]), rest], 1)
    sums[57:64, :] = jnp.zeros((7, LANES), jnp.float32)


def diagonal(block):
    here = lanes((32, 32)) == lax.broadcasted_iota(jnp.int32, (32, 32), 0)
    return jnp.sum(jnp.where(here, block, 0.0), 0, keepdims=True)


def parted(mixed, ends):
    turned = mixed.T
    lane = lanes((32, 32))
    row = lax.broadcasted_iota(jnp.int32, (32, 32), 0)
    upper = jnp.where(lane > row, mixed, turned)
    return jnp.where(lane <= row, mixed, turned), jnp.where(lane == row, ends, upper)


def eliminate(slabs):
    slabs = list(slabs)
    count = len(slabs)
    tile = (8, LANES)
    lane = lanes(tile)
    row = lax.broadcasted_iota(jnp.int32, tile, 0)

    def spread(slab, column):
        return jnp.broadcast_to(slabs[slab][:, column : column + 1], tile)

    ahead = [spread(0, k) for k in range(8)]
    for g in range(count):
        cols = [[ahead[k]] + [spread(i, 8 * g + k) for i in range(g + 1, count)] for k in range(8)]
        ahead = [spread(g + 1, 8 * g + 8 + k) for k in range(8)] if g + 1 < count else []
        for k in range(8):
            here = lane == 8 * g + k
            root = lax.rsqrt(cols[k][0][k : k + 1, :])
            inverse = root * root
            pivot_row = jnp.where(here[:1], 1.0, slabs[g][k : k + 1, :])
            scaled = pivot_row * inverse
            later = [cols[m][0][k : k + 1, :] * inverse for m in range(k + 1, 8)]
            for i in range(count - g):
                factor = cols[k][i]
                if i == 0:
                    factor = jnp.where(row > k, factor, 0.0)
                    kept = jnp.where(here & (row > k), 0.0, slabs[g])
                    slabs[g] = jnp.where(row == k, pivot_row * root, kept - factor * scaled)
                else:
                    slabs[g + i] = jnp.where(here, 0.0, slabs[g + i]) - factor * scaled
                for m in range(k + 1, 8):
                    if i == 0 and m == k + 1:
                        cols[m][i] = cols[m][i] - (factor * cols[m][i][k : k + 1, :]) * inverse
                    else:
                        cols[m][i] = cols[m][i] - factor * later[m - k - 1]
            if ahead:
                below = cols[k][1]
                ahead = [ahead[c] - below * (below[c : c + 1, :] * inverse) for c in range(8)]
    return slabs


def lower_part(slabs, size):
    whole = jnp.concatenate(slabs, 0)
    row = lax.broadcasted_iota(jnp.int32, whole.shape, 0)
    return jnp.where(lanes(whole.shape) <= row, whole, 0.0)[:, :size]


def update(scale, sums, start, fields, new_basis, new_search, values):
    first = sums[0:32, :] * scale
    second = sums[32:64, :] * scale
    mixed, xy, xp, pz = (first[:, 32 * k : 32 * k + 32] for k in range(4))
    other, yp, yz = (
        jnp.concatenate([second[8 * k : 8 * k + 8, 32 * q : 32 * q + 32] for q in range(4)], 0)
        for k in range(3)
    )
    xx, pp = parted(mixed, second[24:25, 0:32])
    yy, pr = parted(other, second[24:25, 32:64])
    px, py, zp = xp.T, yp.T, pz.T
    zero = jnp.zeros((32, 32), jnp.float32)
    gram = [
        jnp.concatenate([xx, xy, xp, zero], 1),
        jnp.concatenate([xy, yy, yp, zero], 1),
        jnp.concatenate([px, py, pp, zero], 1),
    ]
    projected = jnp.concatenate(
        [
            jnp.concatenate([xy, yy, yp], 1),
            jnp.concatenate([yy, yz, zp], 1),
            jnp.concatenate([py, pz, pr], 1),
        ],
        0,
    )
    lower_inv = lower_part(
        eliminate([block[8 * k : 8 * k + 8] for block in gram for k in range(4)]), 96
    )
    half = dot_nn(lower_inv, projected)
    ritz = 0.5 * (dot_nt(half, lower_inv) + dot_nt(lower_inv, half))
    bound = jnp.max(jnp.sum(jnp.abs(ritz), 0, keepdims=True), 1, keepdims=True)
    seed = start[...].astype(jnp.float32)
    moved = bound * seed - dot_nn(seed, ritz)
    square = jnp.concatenate([dot_nt(moved, moved), jnp.zeros((32, 96), jnp.float32)], 1)
    weights = dot_nn(moved, lower_inv)
    quotient = diagonal(xy) / diagonal(xx)
    middle = weights[:, 32:64]
    search_weights = jnp.concatenate([-(middle * quotient), middle, weights[:, 64:96]], 1)
    mixed_fields = dot_nn(jnp.concatenate([weights, search_weights], 0), fields[...])
    mixed_ritz = dot_nn(moved, ritz)
    small_inv = lower_part(eliminate([square[8 * k : 8 * k + 8] for k in range(4)]), 32)
    both = jnp.concatenate([mixed_fields[0:32], mixed_fields[32:64]], 1)
    result = dot_nn(small_inv, both)
    terms = dot_nn(small_inv, moved) * dot_nn(small_inv, mixed_ritz)
    values[...] = dot_nt(jnp.ones((8, 96), jnp.float32), terms)[0:1, :]
    wide = ROWS * LANES
    for s in range(ROWS):
        new_basis[:, s, :] = result[:, LANES * s : LANES * (s + 1)]
        new_search[:, s, :] = result[:, wide + LANES * s : wide + LANES * (s + 1)]


def call(kernel, outs, *args, scratch=(), place=VMEM, cost=None):
    shapes = [jax.ShapeDtypeStruct(shape, jnp.float32) for shape in outs]
    return pl.pallas_call(
        kernel,
        out_shape=shapes,
        in_specs=[place] * len(args),
        cost_estimate=cost,
        out_specs=[VMEM] * len(shapes),
        scratch_shapes=[
            pltpu.VMEM(shape, jnp.float32) if isinstance(shape, tuple) else shape for shape in scratch
        ],
        compiler_params=pltpu.CompilerParams(vmem_limit_bytes=32 * 1024 * 1024),
    )(*args)


def paired(array, axis, first):
    pairs = [(i, i + 1) for i in range(first, lax.axis_size(axis) - 1, 2)]
    return lax.ppermute(array, axis, pairs + [(j, i) for i, j in pairs])


def exchanged(array, axis):
    return lax.all_to_all(array, axis, 0, 0, tiled=True)


def summed(array, count):
    return jnp.sum(array.reshape(count, array.shape[0] // count, LANES), 0)


def total(array):
    across, along = lax.axis_size("gy"), lax.axis_size("gx")
    share = summed(exchanged(array, "gy"), across)
    share = summed(exchanged(jnp.tile(share, (along, 1)), "gx"), along)
    return exchanged(jnp.tile(share, (across, 1)), "gy")


def body(basis, search, conductivity, rotation):
    modes, cells_x, flat = basis.shape
    count = cells_x * flat * lax.axis_size("gx") * lax.axis_size("gy")
    blocks = [basis.shape, search.shape, conductivity.shape]
    rows = call(
        pack_rows,
        [(104, LANES)] * 2,
        *(pltpu.with_memory_space_constraint(x, pltpu.HBM) for x in (basis, search, conductivity)),
        scratch=blocks + [pltpu.SemaphoreType.DMA((3,))],
        place=pl.BlockSpec(memory_space=pltpu.HBM),
    )
    inner_x, inner_p = call(
        inner,
        [(cells_x, modes, flat)] * 2,
        basis,
        search,
        conductivity,
        scratch=[(4, ROWS, LANES)],
        cost=pl.CostEstimate(flops=4 << 20, bytes_accessed=1 << 20, transcendentals=0),
    )
    row_two = paired(rows[1], "gx", 1)
    row_one = paired(rows[0], "gx", 0)
    side_one, side_two, lo, hi = call(
        pack_sides,
        [(112, LANES)] * 2 + [(104, LANES)] * 2,
        basis,
        search,
        conductivity,
        row_two,
        row_one,
        scratch=[(112, LANES)] * 2,
    )
    side_two = paired(side_two, "gy", 1)
    side_one = paired(side_one, "gy", 0)
    fields, sums = call(
        images,
        [(96, ROWS * LANES), (64, LANES)],
        basis,
        search,
        conductivity,
        inner_x,
        inner_p,
        lo,
        hi,
        side_two,
        side_one,
        scratch=[(2, 24, LANES), (2, 5, 16, LANES), (2, 10, MODES, LANES), (160, ROWS * LANES)]
        + [(112, LANES)] * 2,
    )
    sums = total(sums)

    def finish(*refs):
        update(1.0 / count, *refs)

    new_basis, new_search, values = call(
        finish,
        [(modes, cells_x, flat), (modes, cells_x, flat), (1, modes)],
        sums,
        rotation.T,
        fields,
    )
    return new_basis, new_search, values.reshape(modes)


def solution(mesh):
    in_specs = (P(None, "gx", "gy"), P(None, "gx", "gy"), P("gx", "gy"), P())
    out_specs = (P(None, "gx", "gy"), P(None, "gx", "gy"), P())
    return jax.shard_map(body, mesh=mesh, in_specs=in_specs, out_specs=out_specs, check_vma=False)
```
